256 devices in a mesh: pp: 16 (over z_hi, y), ep: 16 (over x, z_lo, core).
Axes of the slice: x: 4, y: 4, z: 8 (z_hi: 4, z_lo: 2; z = z_hi * 2 + z_lo), core: 2. Of those that a mesh axis runs over, the one named last changes fastest.
Arguments:
- stream_up: bfloat16 [16, 1024, 7168], P('pp', 'ep'), may hold values from -6 to 6
- stream_down: bfloat16 [16, 1024, 7168], P('pp', 'ep'), may hold values from -6 to 6
- norm_gain: bfloat16 [16, 7168], P('pp'), may hold values from 0.099609375 to 1.8984375
- router: bfloat16 [16, 7168, 2], P('pp'), may hold values from -0.0625 to 0.0625
- w_gate: bfloat16 [16, 7168, 2048], P('pp', None, 'ep'), may hold values from -0.0625 to 0.0625
- w_up: bfloat16 [16, 7168, 2048], P('pp', None, 'ep'), may hold values from -0.0625 to 0.0625
- w_down: bfloat16 [16, 2048, 7168], P('pp', 'ep'), may hold values from -0.1875 to 0.1875
- routes_up: int32 [1, 16, 1024, 1], P(None, 'pp', 'ep'), may hold values from 0 to 1; in each aligned block of 64 rows (0 to 63, 64 to 127, ..., all dimensions but the last counted through in order) at most 32 rows name the same one
- routes_down: int32 [1, 16, 1024, 1], P(None, 'pp', 'ep'), may hold values from 0 to 1; in each aligned block of 64 rows (0 to 63, 64 to 127, ..., all dimensions but the last counted through in order) at most 32 rows name the same one
Outputs:
- rising: bfloat16 [16, 1024, 7168], P('pp', 'ep')
- falling: bfloat16 [16, 1024, 7168], P('pp', 'ep')
The draws below stay inside these ranges and needn't reach their ends.
Inputs may be any that keep to these rules, and one draw needn't show every extreme that they name: `routes_up`: among the 64 tokens of one device at one section and pass, no expert is chosen more than 32 times; some such group reaches 32. `routes_down`: among the 64 tokens of one device at one section and pass, no expert is chosen more than 32 times; some such group reaches 32.
All inputs are finite; a program needn't handle non-finite values.
Results may differ from the reference program's by a relative error of at most 0.0058.
Values may be sent and summed in bfloat16 or wider, within the bound.
A program may use at most 128 MiB of HBM per device.

```python
import math
import jax
import jax.numpy as jnp
import numpy as np
from jax import lax

D = 7168
EXP_HID = 1024
EXPERTS = 2
TICKS = 1
STREAM_TOK = 64
SECTIONS = 16
TOKENS = 1024
CAP = 32
N_EP = 16


def block_scale(own_key, shape, pieces, smallest, top_value):
    def one(dim, blocks):
        steps = jax.random.uniform(jax.random.fold_in(jax.random.fold_in(own_key, 6), dim), (blocks,), jnp.float32, smallest / len(pieces), top_value / len(pieces))
        return jnp.repeat(jnp.exp(steps), shape[dim] // blocks).reshape((-1,) + (1,) * (len(shape) - dim - 1))

    level = one(*pieces[0])
    for cut in pieces[1:]:
        level = level * one(*cut)
    return level


def shared_out(stream_key, own, number, rows, number_of, top, limit, lean):
    sequence = jax.random.permutation(stream_key, number_of)
    crowded, ordinary = portions_of(number_of, rows * top, limit, lean, True), portions_of(number_of, rows * top, limit, lean, False)
    places = jnp.arange(number_of)

    def named(tallies, offset_by):
        used = int((tallies > 0).sum())
        fixed = max(1, used // 4)
        passed = fixed + (places - fixed + offset_by * (used - fixed)) % max(1, number_of - fixed)
        return jnp.zeros((number_of,), jnp.int32).at[sequence[jnp.where(places < fixed, places, passed)]].set(jnp.asarray(tallies, jnp.int32))

    tallies = jnp.where(number % 4 == 0, named(crowded, number // 4), named(ordinary, number - number // 4 - 1))
    mixed = jax.random.permutation(jax.random.fold_in(own, 3), number_of)
    source_of, sink = mixed[0:number_of // 2 * 2:2], mixed[1:number_of // 2 * 2:2]
    margin = jnp.minimum(tallies[source_of] - 1, limit - tallies[sink]) // 2
    margin = jnp.where((source_of == sequence[0]) | (sink == sequence[0]) | (tallies[sink] == 0), 0, jnp.maximum(margin, 0))
    passed = jax.random.randint(jax.random.fold_in(own, 4), (number_of // 2,), 0, 1 << 20) % (margin + 1)
    tallies = tallies.at[source_of].add(-passed).at[sink].add(passed)
    labels = jnp.searchsorted(jnp.cumsum(tallies), jnp.arange(rows * top), side="right").astype(jnp.int32)
    table = labels.reshape(top, rows).T
    table = table[jax.random.permutation(jax.random.fold_in(own, 1), rows)]
    offset_by = jax.random.randint(jax.random.fold_in(own, 2), (rows, 1), 0, top)
    return jnp.take_along_axis(table, (jnp.arange(top)[None, :] + offset_by) % top, axis=1)


def portions_of(count, total, most, lean, full):
    portions = [(1 << 20) // math.isqrt(standing ** lean) + 1 for standing in range(1, count + 1)]
    largest = most if full else min(most, max(-(-total // count), total * portions[0] // sum(portions)))
    least = 1 if total - largest >= count - 1 else 0
    counts, surplus = [largest] + [least] * (count - 1), total - largest - least * (count - 1)
    while surplus > 0:
        candidates = [i for i in range(1, count) if counts[i] < largest] or [i for i in range(1, count) if counts[i] < most]
        pool, left = sum([portions[i] for i in candidates]), surplus
        for i in candidates:
            addition = min(most - counts[i], max(1, left * portions[i] // pool), surplus)
            counts[i] = counts[i] + addition
            surplus = surplus - addition
    return np.array(counts)


def centred(own_key, shape, scale, limit, split=(), kind=jnp.bfloat16):
    array = scale * jax.random.normal(own_key, shape, jnp.float32)
    if split:
        array = array * block_scale(own_key, shape, split, -0.22, 0.18)
    return jnp.clip(array, -limit, limit).astype(kind)


def setup_inputs(seed: int = 0) -> dict:
    keys = jax.random.split(jax.random.key(seed), 10)
    stream_up = centred(keys[0], (SECTIONS, TOKENS, D), 1.0, 6.0, ((0, 16), (1, 16)))
    stream_down = centred(keys[1], (SECTIONS, TOKENS, D), 1.0, 6.0, ((0, 16), (1, 16)))
    norm_gain = jnp.clip(1.0 + 0.18 * jax.random.normal(keys[2], (SECTIONS, D), jnp.float32), 0.099609375, 1.8984375).astype(jnp.bfloat16)
    router = centred(keys[3], (SECTIONS, D, EXPERTS), D ** -0.5, 0.0625, ((0, 16),))
    w_gate = centred(keys[4], (SECTIONS, D, EXPERTS * EXP_HID), D ** -0.5, 0.0625, ((0, 16), (2, 16)))
    w_up = centred(keys[5], (SECTIONS, D, EXPERTS * EXP_HID), D ** -0.5, 0.0625, ((0, 16), (2, 16)))
    w_down = centred(keys[6], (SECTIONS, EXPERTS * EXP_HID, D), EXP_HID ** -0.5, 0.1875, ((0, 16), (1, 16)))
    routes_up_keys = jax.random.split(jax.random.fold_in(keys[7], 1), TICKS * SECTIONS * TOKENS // STREAM_TOK)
    routes_up_turns = jax.random.permutation(jax.random.fold_in(keys[7], 3), TICKS * SECTIONS * TOKENS // STREAM_TOK)
    routes_up = jax.vmap(lambda own, number: shared_out(jax.random.fold_in(keys[7], 2), own, number, STREAM_TOK, EXPERTS, 1, CAP, 0))(routes_up_keys, routes_up_turns).reshape((TICKS, SECTIONS, TOKENS, 1))
    routes_down_keys = jax.random.split(jax.random.fold_in(keys[8], 1), TICKS * SECTIONS * TOKENS // STREAM_TOK)
    routes_down_turns = jax.random.permutation(jax.random.fold_in(keys[8], 3), TICKS * SECTIONS * TOKENS // STREAM_TOK)
    routes_down = jax.vmap(lambda own, number: shared_out(jax.random.fold_in(keys[8], 2), own, number, STREAM_TOK, EXPERTS, 1, CAP, 0))(routes_down_keys, routes_down_turns).reshape((TICKS, SECTIONS, TOKENS, 1))
    return {"stream_up": stream_up, "stream_down": stream_down, "norm_gain": norm_gain, "router": router, "w_gate": w_gate, "w_up": w_up, "w_down": w_down, "routes_up": routes_up, "routes_down": routes_down}


EPSILON = 1e-06
ROUTE_SCALE = 2.5

def one_section(tokens_in, gain_vec, router, w_gate, w_up, w_down, chosen):
    group_size = N_EP // EXPERTS
    hid_device = EXP_HID // group_size
    widened = tokens_in.astype(jnp.float32)
    normed = (widened * lax.rsqrt(lax.optimization_barrier(jnp.mean(widened * widened, axis=1, keepdims=True)) + EPSILON) * gain_vec.astype(jnp.float32)).astype(jnp.bfloat16)
    affinity = jax.nn.sigmoid(jnp.dot(normed, router, preferred_element_type=jnp.float32))
    expert_ids = jnp.arange(EXPERTS).astype(jnp.int32)
    is_member = chosen.astype(jnp.int32)[:, None] == expert_ids[None, :]
    weight = ROUTE_SCALE * lax.optimization_barrier(jnp.sum(jnp.where(is_member, affinity, jnp.zeros_like(affinity)), axis=1))
    output = jnp.zeros(widened.shape, jnp.float32)
    for expert in range(EXPERTS):
        start = expert * EXP_HID
        gate_act = jnp.dot(normed, w_gate[:, start:start + EXP_HID], preferred_element_type=jnp.float32)
        up_act = jnp.dot(normed, w_up[:, start:start + EXP_HID], preferred_element_type=jnp.float32)
        hidden = (jax.nn.silu(gate_act) * up_act).astype(jnp.bfloat16)
        result = jnp.zeros(widened.shape, jnp.float32)
        for piece_num in range(group_size):
            lower = piece_num * hid_device
            partial_value = jnp.dot(hidden[:, lower:lower + hid_device], w_down[start + lower:start + lower + hid_device], preferred_element_type=jnp.float32).astype(jnp.bfloat16)
            result = result + lax.optimization_barrier(partial_value).astype(jnp.float32)
        output = jnp.where(is_member[:, expert:expert + 1], result, output)
    return (widened + weight[:, None] * output).astype(jnp.bfloat16)

def apply_sections(states, norm_gain, router, w_gate, w_up, w_down, routes):

    def single(items):
        return one_section(items[0], items[1], items[2], items[3], items[4], items[5], items[6])
    return lax.map(single, (states, norm_gain, router, w_gate, w_up, w_down, routes[:, :, 0]))

def reference(stream_up, stream_down, norm_gain, router, w_gate, w_up, w_down, routes_up, routes_down):
    rising = stream_up
    falling = stream_down
    for tick_num in range(TICKS):
        rising = jnp.roll(apply_sections(rising, norm_gain, router, w_gate, w_up, w_down, routes_up[tick_num]), 1, axis=0)
        falling = jnp.roll(apply_sections(falling, norm_gain, router, w_gate, w_up, w_down, routes_down[tick_num]), -1, axis=0)
    return (rising, falling)
```

```python
import jax
import jax.numpy as jnp
from jax import lax
from jax.experimental import pallas as pl
from jax.experimental.pallas import tpu as pltpu
from jax.sharding import PartitionSpec as P

MESH = pl.DeviceIdType.MESH
F32 = jnp.float32
BF16 = jnp.bfloat16
EPSILON = 1e-06
ROUTE_SCALE = 2.5

D = 7168
ROWS = 64
HID = 128
HALF = D // 2
KC = 1024
NK = D // KC
JC = 512
NJ = HALF // JC
KX = 5

OWN, Z_OWN, ENT, Z_ENT, X_OWN, D_OWN, X_ENT, D_ENT = range(8)

OWN_X, OWN_Z, CROSS, ENT_X, ENT_Z, FWD_OWN, FWD_ENT = range(0, 7 * NK, NK)
W_BASE = 7 * NK
WD_Z, WD_RELAY, WD_CORE, WG_CORE, WU_CORE = range(W_BASE, W_BASE + 5)
ACT_Z = W_BASE + 5
R_BASE = ACT_Z + 4
RET_XO, RET_XE, RET_ZO, RET_ZE, RET_C, RET_CF = range(R_BASE, R_BASE + 6 * NJ, NJ)
OUT_UP = R_BASE + 6 * NJ
OUT_DN = OUT_UP + 2 * NJ
N_SEM = OUT_DN + 2 * NJ


def dot(a, b):
    return jnp.dot(a, b, preferred_element_type=F32)


def kernel(
    up_ref, down_ref, gain_ref, router_ref, wg_ref, wu_ref, wd_ref, routes_ref,
    out_up, out_dn,
    xin, xb, fb, wg, wu, wd, actm, actz, acc, sx, rx, sz, sc, rze, fa, fz, outb,
    place, place_t, weight, local_sem, send_sem, recv_sem,
):
    pp = lax.axis_index("pp")
    ep = lax.axis_index("ep")
    n_pp = lax.axis_size("pp")
    xi = ep // 4
    zi = (ep // 2) % 2
    ci = ep % 2

    def device(x, z, c):
        return (pp, x * 4 + z * 2 + c)

    xn = device(xi + 1 - 2 * (xi % 2), zi, ci)
    zn = device(xi, 1 - zi, ci)
    xc = device(3 - xi, zi, ci)
    core = device(xi, zi, 1 - ci)
    above = (lax.rem(pp + 1, n_pp), ep)
    below = (lax.rem(pp + n_pp - 1, n_pp), ep)
    expert = xi // 2
    my_half = zi * HALF
    other_half = (1 - zi) * HALF

    def remote(src, dst, index, to):
        return pltpu.make_async_remote_copy(
            src_ref=src,
            dst_ref=dst,
            send_sem=send_sem.at[index],
            recv_sem=recv_sem.at[index],
            device_id=to,
            device_id_type=MESH,
        )

    def cols(k):
        return pl.ds(pl.multiple_of(k * KC, KC), KC)

    def block(slot, k):
        return xb.at[slot, :, cols(k)]

    def own_x(k):
        return remote(block(OWN, k), block(X_OWN, k), OWN_X + k, xn)

    def own_z(k):
        return remote(block(OWN, k), block(Z_OWN, k), OWN_Z + k, zn)

    def cross(k):
        return remote(fb.at[:, cols(k)], block(ENT, k), CROSS + k, xc)

    def ent_x(k):
        return remote(block(ENT, k), block(X_ENT, k), ENT_X + k, xn)

    def ent_z(k):
        return remote(block(ENT, k), block(Z_ENT, k), ENT_Z + k, zn)

    def fwd_own(k):
        return remote(block(Z_OWN, k), block(D_OWN, k), FWD_OWN + k, xn)

    def fwd_ent_x(k):
        return remote(block(Z_ENT, k), block(D_ENT, k), FWD_ENT + k, xn)

    def fwd_ent_z(k):
        return remote(block(X_ENT, k), block(D_ENT, k), FWD_ENT + k, zn)

    half_mine = pl.ds(pl.multiple_of(my_half, HALF), HALF)
    half_other = pl.ds(pl.multiple_of(other_half, HALF), HALF)
    wd_z = remote(wd_ref.at[:, half_other], wd.at[2], WD_Z, zn)
    wd_relay = remote(wd.at[2], wd.at[3], WD_RELAY, core)
    wd_core = remote(wd_ref.at[:, half_mine], wd.at[1], WD_CORE, core)
    wg_core = remote(wg_ref, wg.at[1], WG_CORE, core)
    wu_core = remote(wu_ref, wu.at[1], WU_CORE, core)

    def act_z(pair):
        rows = pl.ds(pair * 2 * ROWS, 2 * ROWS)
        return remote(actm.at[rows], actz.at[rows], ACT_Z + pair, zn)

    def ret_xo(j):
        return remote(sx.at[j, pl.ds(0, 128)], rx.at[j, pl.ds(0, 128)], RET_XO + j, xn)

    def ret_xe(j):
        return remote(sx.at[j, pl.ds(128, 128)], rx.at[j, pl.ds(128, 128)], RET_XE + j, xn)

    def ret_zo(j):
        return remote(sz.at[j, pl.ds(0, ROWS)], fz.at[j, pl.ds(0, ROWS)], RET_ZO + j, zn)

    def ret_ze(j):
        return remote(sz.at[j, pl.ds(ROWS, ROWS)], rze.at[j], RET_ZE + j, zn)

    def ret_c(j):
        return remote(sc.at[j], fa.at[j, pl.ds(ROWS, ROWS)], RET_C + j, xc)

    def ret_cf(j):
        return remote(rze.at[j], fz.at[j, pl.ds(ROWS, ROWS)], RET_CF + j, xc)

    def out_cols(j, part):
        start = (my_half if part == 0 else other_half) + j * JC
        return pl.ds(pl.multiple_of(start, JC), JC)

    def send_up(j, part):
        where = out_cols(j, part)
        return remote(
            outb.at[j, part, pl.ds(0, ROWS)], out_up.at[:, where], OUT_UP + 2 * j + part, above
        )

    def send_dn(j, part):
        where = out_cols(j, part)
        return remote(
            outb.at[j, part, pl.ds(ROWS, ROWS)], out_dn.at[:, where], OUT_DN + 2 * j + part, below
        )

    def loop(count, body):
        def step(k, carry):
            body(k)
            return carry

        lax.fori_loop(0, count, step, 0)

    load_up = pltpu.make_async_copy(up_ref, xin.at[pl.ds(0, ROWS)], local_sem.at[0])
    load_dn = pltpu.make_async_copy(down_ref, xin.at[pl.ds(ROWS, ROWS)], local_sem.at[1])
    load_wg = pltpu.make_async_copy(wg_ref, wg.at[0], local_sem.at[2])
    load_wu = pltpu.make_async_copy(wu_ref, wu.at[0], local_sem.at[3])
    load_wd = pltpu.make_async_copy(wd_ref.at[:, half_mine], wd.at[0], local_sem.at[4])
    load_up.start()
    load_dn.start()
    barrier = pltpu.get_barrier_semaphore()
    for to in (xn, zn, xc, core, above, below):
        pl.semaphore_signal(barrier, inc=1, device_id=to, device_id_type=MESH)
    load_wg.start()
    load_wu.start()
    load_wd.start()

    token_r = lax.broadcasted_iota(jnp.int32, (128, 128), 0)
    token_c = lax.broadcasted_iota(jnp.int32, (128, 128), 1)
    chosen = jnp.broadcast_to(routes_ref[...], (128, 128))
    mine = (chosen == expert).astype(F32)
    before = ((token_r < token_c) & (token_r // 64 == token_c // 64)).astype(F32)
    ahead = dot(mine.astype(BF16), before.astype(BF16))
    inside = (token_c % 64).astype(F32)
    stream = (token_c // 64 * 32).astype(F32)
    target = stream + jnp.where(mine > 0.5, ahead, 64.0 + inside - ahead)
    hit = (token_r.astype(F32) == target).astype(F32)
    place[...] = hit.astype(BF16)
    place_t[...] = hit.T.astype(BF16)

    load_up.wait()
    load_dn.wait()

    def squares(k, total):
        part = xin[:, cols(k)].astype(F32)
        return total + jnp.sum(part * part, axis=1, keepdims=True)

    total = lax.fori_loop(0, NK, squares, jnp.zeros((128, 1), F32))
    inverse = lax.rsqrt(total * (1.0 / D) + EPSILON)
    weight[...] = jnp.broadcast_to(inverse, (128, 128))

    def normed(k):
        gain = gain_ref[:, cols(k)].astype(F32)
        return (xin[:, cols(k)].astype(F32) * weight[:, 0:1] * gain).astype(BF16)

    pl.semaphore_wait(barrier, 6)

    def first(k):
        moved = dot(place[...], normed(k)).astype(BF16)
        xb[OWN, :, cols(k)] = moved[:ROWS]
        fb[:, cols(k)] = moved[ROWS:]
        cross(k).start()
        own_x(k).start()
        own_z(k).start()

    loop(NK, first)
    wg_core.start()
    wu_core.start()
    wd_core.start()

    def affinity(k, carry):
        zero, one = carry
        part = normed(k).astype(F32)
        near = router_ref[:, cols(k)].astype(F32)
        zero = zero + jnp.sum(part * near[0:1], axis=1, keepdims=True)
        one = one + jnp.sum(part * near[1:2], axis=1, keepdims=True)
        return zero, one

    empty = jnp.zeros((128, 1), F32)
    zero, one = lax.fori_loop(0, NK, affinity, (empty, empty))
    named = jnp.where(token_r == token_c, chosen, 0).astype(F32)
    named = jnp.sum(named, axis=1, keepdims=True)
    logit = jnp.where(named > 0.5, one, zero)
    weight[...] = jnp.broadcast_to(ROUTE_SCALE * jax.nn.sigmoid(logit), (128, 128))

    load_wg.wait()
    load_wu.wait()
    load_wd.wait()
    wg_core.wait_recv()
    wu_core.wait_recv()

    def hidden_step(pair, k):
        rows = xb[pl.ds(2 * pair, 2), :, cols(k)].reshape(2 * ROWS, KC)
        gate = dot(rows, jnp.concatenate([wg[0, cols(k)], wg[1, cols(k)]], axis=1))
        up = dot(rows, jnp.concatenate([wu[0, cols(k)], wu[1, cols(k)]], axis=1))
        first_one = k == 0
        acc[:, 0:256] = jnp.where(first_one, 0.0, acc[:, 0:256]) + gate
        acc[:, 256:512] = jnp.where(first_one, 0.0, acc[:, 256:512]) + up

    def hidden_end(pair):
        act = jax.nn.silu(acc[:, 0:256]) * acc[:, 256:512]
        actm[pl.ds(pair * 2 * ROWS, 2 * ROWS)] = act.astype(BF16)
        act_z(pair).start()

    acc[...] = jnp.zeros_like(acc)

    def second(k):
        cross(k).wait_recv()
        ent_x(k).start()
        ent_z(k).start()
        own_z(k).wait_recv()
        fwd_own(k).start()
        hidden_step(0, k)

    loop(NK, second)
    wd_z.start()
    hidden_end(0)

    def third(k):
        ent_z(k).wait_recv()

        @pl.when(k < KX)
        def _():
            fwd_ent_x(k).start()

        hidden_step(1, k)

    loop(NK, third)
    hidden_end(1)

    def fourth(k):
        own_x(k).wait_recv()
        fwd_own(k).wait_recv()
        hidden_step(2, k)

    loop(NK, fourth)
    hidden_end(2)

    def relay(k):
        ent_x(k).wait_recv()

        @pl.when(k >= KX)
        def _():
            fwd_ent_z(k).start()

    loop(NK, relay)
    wd_z.wait_recv()
    wd_relay.start()
    wd_core.wait_recv()

    def back(pair, j):
        at = pl.ds(pl.multiple_of(j * JC, JC), JC)
        base = pair * 2 * ROWS
        far = jnp.concatenate([actz[base + ROWS:base + 2 * ROWS], actz[base:base + ROWS]], axis=0)
        left = jnp.concatenate([actm[base:base + 2 * ROWS], far], axis=1)
        return dot(left, wd[:, :, at].reshape(4 * HID, JC))

    def back_o(j):
        sx[j, 0:128] = back(2, j).astype(BF16)
        ret_xo(j).start()

    def back_e(j):
        sx[j, 128:256] = back(3, j).astype(BF16)
        ret_xe(j).start()

    def fifth(k):
        fwd_ent_x(k).wait_recv()
        hidden_step(3, k)

    loop(KX, fifth)
    act_z(2).wait_recv()
    wd_relay.wait_recv()
    loop(3, back_o)

    def sixth(k):
        fwd_ent_z(k + KX).wait_recv()
        hidden_step(3, k + KX)

    loop(NK - KX, sixth)
    hidden_end(3)

    act_z(3).wait_recv()

    def pieces(j):
        @pl.when(j >= 3)
        def _():
            back_o(j)

        back_e(j)

    loop(NJ, pieces)
    act_z(0).wait_recv()
    act_z(1).wait_recv()

    def drain(k):
        own_x(k).wait_send()
        own_z(k).wait_send()
        cross(k).wait_send()
        ent_x(k).wait_send()
        ent_z(k).wait_send()
        fwd_own(k).wait_send()
        fwd_ent_x(k).wait_send()

    loop(NK, drain)
    for copy in (wd_z, wd_relay, wd_core, wg_core, wu_core, act_z(0), act_z(1), act_z(2), act_z(3)):
        copy.wait_send()

    def sums(j):
        near = back(0, j)
        ret_xo(j).wait_recv()
        near = near + rx[j, 0:128].astype(F32)
        sz[j, 0:ROWS] = near[ROWS:].astype(BF16)
        ret_zo(j).start()
        fa[j, 0:ROWS] = near[:ROWS].astype(BF16)
        far = back(1, j)
        ret_xe(j).wait_recv()
        far = far + rx[j, 128:256].astype(F32)
        sz[j, ROWS:128] = far[ROWS:].astype(BF16)
        ret_ze(j).start()
        sc[j] = far[:ROWS].astype(BF16)
        ret_c(j).start()

    def onward(j):
        ret_ze(j).wait_recv()
        ret_cf(j).start()

    def finish(j, part, held):
        mixed = dot(place_t[...], held[j])
        out = xin[:, out_cols(j, part)].astype(F32) + weight[:, 0:1] * mixed
        outb[j, part] = out.astype(BF16)
        send_up(j, part).start()
        send_dn(j, part).start()

    def final(j):
        ret_c(j).wait_recv()
        finish(j, 0, fa)
        ret_zo(j).wait_recv()
        ret_cf(j).wait_recv()
        finish(j, 1, fz)

    def tail(i):
        @pl.when(i < NJ)
        def _():
            sums(i)

        @pl.when((i >= 1) & (i < NJ + 1))
        def _():
            onward(i - 1)

        @pl.when(i >= 2)
        def _():
            final(i - 2)

    loop(NJ + 2, tail)

    def last(j):
        ret_xo(j).wait_send()
        ret_xe(j).wait_send()
        ret_zo(j).wait_send()
        ret_ze(j).wait_send()
        ret_c(j).wait_send()
        ret_cf(j).wait_send()
        for part in range(2):
            send_up(j, part).wait_send()
            send_dn(j, part).wait_send()
            send_up(j, part).wait_recv()
            send_dn(j, part).wait_recv()

    loop(NJ, last)


def local(stream_up, stream_down, norm_gain, router, w_gate, w_up, w_down, routes_up, routes_down):
    routes = jnp.concatenate([routes_up[0, 0, :, 0], routes_down[0, 0, :, 0]])[None]
    any_spec = pl.BlockSpec(memory_space=pl.ANY)
    vmem_spec = pl.BlockSpec(memory_space=pltpu.VMEM)
    out = jax.ShapeDtypeStruct((ROWS, D), BF16)
    rising, falling = pl.pallas_call(
        kernel,
        out_shape=(out, out),
        in_specs=[any_spec, any_spec, vmem_spec, vmem_spec, any_spec, any_spec, any_spec, vmem_spec],
        out_specs=(any_spec, any_spec),
        scratch_shapes=[
            pltpu.VMEM((128, D), BF16),
            pltpu.VMEM((8, ROWS, D), BF16),
            pltpu.VMEM((ROWS, D), BF16),
            pltpu.VMEM((2, D, HID), BF16),
            pltpu.VMEM((2, D, HID), BF16),
            pltpu.VMEM((4, HID, HALF), BF16),
            pltpu.VMEM((8 * ROWS, 2 * HID), BF16),
            pltpu.VMEM((8 * ROWS, 2 * HID), BF16),
            pltpu.VMEM((2 * ROWS, 4 * HID), F32),
            pltpu.VMEM((NJ, 4 * ROWS, JC), BF16),
            pltpu.VMEM((NJ, 4 * ROWS, JC), BF16),
            pltpu.VMEM((NJ, 2 * ROWS, JC), BF16),
            pltpu.VMEM((NJ, ROWS, JC), BF16),
            pltpu.VMEM((NJ, ROWS, JC), BF16),
            pltpu.VMEM((NJ, 2 * ROWS, JC), BF16),
            pltpu.VMEM((NJ, 2 * ROWS, JC), BF16),
            pltpu.VMEM((NJ, 2, 2 * ROWS, JC), BF16),
            pltpu.VMEM((128, 128), BF16),
            pltpu.VMEM((128, 128), BF16),
            pltpu.VMEM((128, 128), F32),
            pltpu.SemaphoreType.DMA((5,)),
            pltpu.SemaphoreType.DMA((N_SEM,)),
            pltpu.SemaphoreType.DMA((N_SEM,)),
        ],
        compiler_params=pltpu.CompilerParams(
            collective_id=0, has_side_effects=True, vmem_limit_bytes=48 * 2**20
        ),
        name="relay",
    )(
        stream_up[0], stream_down[0], norm_gain, router[0].T, w_gate[0], w_up[0], w_down[0], routes
    )
    return rising[None], falling[None]


def solution(mesh):
    placed = (
        P("pp", "ep", None),
        P("pp", "ep", None),
        P("pp", None),
        P("pp", None, None),
        P("pp", None, "ep"),
        P("pp", None, "ep"),
        P("pp", "ep", None),
        P(None, "pp", "ep", None),
        P(None, "pp", "ep", None),
    )
    return jax.shard_map(
        local,
        mesh=mesh,
        in_specs=placed,
        out_specs=(P("pp", "ep", None), P("pp", "ep", None)),
        check_vma=False,
    )
```

```python
import jax
import jax.numpy as jnp
from jax import lax
from jax.experimental import pallas as pl
from jax.experimental.pallas import tpu as pltpu
from jax.sharding import PartitionSpec as P

MESH = pl.DeviceIdType.MESH
F32 = jnp.float32
BF16 = jnp.bfloat16
EPSILON = 1e-06
ROUTE_SCALE = 2.5

D = 7168
ROWS = 64
HID = 128
HALF = D // 2
KC = 1024
NK = D // KC
JC = 512
NJ = HALF // JC
KX = 5

OWN, Z_OWN, ENT, Z_ENT, X_OWN, D_OWN, X_ENT, D_ENT = range(8)

OWN_X, OWN_Z, CROSS, ENT_X, ENT_Z, FWD_OWN, FWD_ENT = range(0, 7 * NK, NK)
W_BASE = 7 * NK
WD_Z, WD_RELAY, WD_CORE, WG_CORE, WU_CORE = range(W_BASE, W_BASE + 5)
ACT_Z = W_BASE + 5
R_BASE = ACT_Z + 4
RET_XO, RET_XE, RET_ZO, RET_ZC, RET_C = range(R_BASE, R_BASE + 5 * NJ, NJ)
OUT_UP = R_BASE + 5 * NJ
OUT_DN = OUT_UP + 2 * NJ
RELAY_UP = OUT_DN + 2 * NJ
RELAY_DN = RELAY_UP + NJ
N_SEM = RELAY_DN + NJ


def dot(a, b):
    return jnp.dot(a, b, preferred_element_type=F32)


def kernel(
    up_ref, down_ref, gain_ref, router_ref, wg_ref, wu_ref, wd_ref, routes_up, routes_down,
    out_up, out_dn,
    xin, gain_vm, router_vm, routes_vm, xb, fb, wg, wu, wd, actm, actz, acc, sx, rx, sz, sc, fa, fz, outb,
    relay_up, relay_dn, place, place_t, weight, local_sem, send_sem, recv_sem,
):
    pp = lax.axis_index("pp")
    ep = lax.axis_index("ep")
    n_pp = lax.axis_size("pp")
    xi = ep // 4
    zi = (ep // 2) % 2
    ci = ep % 2

    def device(x, z, c):
        return (pp, x * 4 + z * 2 + c)

    xn = device(xi + 1 - 2 * (xi % 2), zi, ci)
    zn = device(xi, 1 - zi, ci)
    xc = device(3 - xi, zi, ci)
    xc_zn = device(3 - xi, 1 - zi, ci)
    core = device(xi, zi, 1 - ci)
    above = (lax.rem(pp + 1, n_pp), ep)
    below = (lax.rem(pp + n_pp - 1, n_pp), ep)
    expert = xi // 2

    yi = pp % 4
    low = yi == 0
    high = yi == 3
    across = (jnp.where(low, pp + 3, lax.rem(pp + n_pp - 3, n_pp)), ep)
    next_row = (lax.rem(pp + 4, n_pp), ep)
    last_row = (lax.rem(pp + n_pp - 4, n_pp), ep)
    my_half = zi * HALF
    other_half = (1 - zi) * HALF

    def remote(src, dst, index, to):
        return pltpu.make_async_remote_copy(
            src_ref=src,
            dst_ref=dst,
            send_sem=send_sem.at[index],
            recv_sem=recv_sem.at[index],
            device_id=to,
            device_id_type=MESH,
        )

    def cols(k):
        return pl.ds(pl.multiple_of(k * KC, KC), KC)

    def block(slot, k):
        return xb.at[slot, :, cols(k)]

    def own_x(k):
        return remote(block(OWN, k), block(X_OWN, k), OWN_X + k, xn)

    def own_z(k):
        return remote(block(OWN, k), block(Z_OWN, k), OWN_Z + k, zn)

    def cross(k):
        return remote(fb.at[:, cols(k)], block(ENT, k), CROSS + k, xc)

    def ent_x(k):
        return remote(block(ENT, k), block(X_ENT, k), ENT_X + k, xn)

    def ent_z(k):
        return remote(block(ENT, k), block(Z_ENT, k), ENT_Z + k, zn)

    def fwd_own(k):
        return remote(block(Z_OWN, k), block(D_OWN, k), FWD_OWN + k, xn)

    def fwd_ent_x(k):
        return remote(block(Z_ENT, k), block(D_ENT, k), FWD_ENT + k, xn)

    def fwd_ent_z(k):
        return remote(block(X_ENT, k), block(D_ENT, k), FWD_ENT + k, zn)

    half_mine = pl.ds(pl.multiple_of(my_half, HALF), HALF)
    half_other = pl.ds(pl.multiple_of(other_half, HALF), HALF)
    wd_z = remote(wd_ref.at[:, half_other], wd.at[2], WD_Z, zn)
    wd_relay = remote(wd.at[2], wd.at[3], WD_RELAY, core)
    wd_core = remote(wd_ref.at[:, half_mine], wd.at[1], WD_CORE, core)
    wg_core = remote(wg_ref, wg.at[1], WG_CORE, core)
    wu_core = remote(wu_ref, wu.at[1], WU_CORE, core)

    def act_z(pair):
        rows = pl.ds(pair * 2 * ROWS, 2 * ROWS)
        return remote(actm.at[rows], actz.at[rows], ACT_Z + pair, zn)

    def ret_xo(j):
        return remote(sx.at[j, pl.ds(0, 128)], rx.at[j, pl.ds(0, 128)], RET_XO + j, xn)

    def ret_xe(j):
        return remote(sx.at[j, pl.ds(128, 128)], rx.at[j, pl.ds(128, 128)], RET_XE + j, xn)

    def ret_zo(j):
        return remote(sz.at[j, pl.ds(0, ROWS)], fz.at[j, pl.ds(0, ROWS)], RET_ZO + j, zn)

    def ret_zc(j):
        return remote(sz.at[j, pl.ds(ROWS, ROWS)], fz.at[j, pl.ds(ROWS, ROWS)], RET_ZC + j, xc_zn)

    def ret_c(j):
        return remote(sc.at[j], fa.at[j, pl.ds(ROWS, ROWS)], RET_C + j, xc)

    def out_cols(j, part):
        start = (my_half if part == 0 else other_half) + j * JC
        return pl.ds(pl.multiple_of(start, JC), JC)

    def send_up(j, part):
        where = out_cols(j, part)
        return remote(
            outb.at[j, part, pl.ds(0, ROWS)], out_up.at[:, where], OUT_UP + 2 * j + part, above
        )

    def send_dn(j, part):
        where = out_cols(j, part)
        return remote(
            outb.at[j, part, pl.ds(ROWS, ROWS)], out_dn.at[:, where], OUT_DN + 2 * j + part, below
        )

    def detour_up(j):
        return remote(outb.at[j, 0, pl.ds(0, ROWS)], relay_up.at[j], RELAY_UP + j, across)

    def detour_dn(j):
        return remote(outb.at[j, 0, pl.ds(ROWS, ROWS)], relay_dn.at[j], RELAY_DN + j, across)

    def onward_up(j):
        return pltpu.make_async_remote_copy(
            src_ref=relay_up.at[j],
            dst_ref=out_up.at[:, out_cols(j, 0)],
            send_sem=send_sem.at[RELAY_UP + j],
            recv_sem=recv_sem.at[OUT_UP + 2 * j],
            device_id=next_row,
            device_id_type=MESH,
        )

    def onward_dn(j):
        return pltpu.make_async_remote_copy(
            src_ref=relay_dn.at[j],
            dst_ref=out_dn.at[:, out_cols(j, 0)],
            send_sem=send_sem.at[RELAY_DN + j],
            recv_sem=recv_sem.at[OUT_DN + 2 * j],
            device_id=last_row,
            device_id_type=MESH,
        )

    def loop(count, body):
        def step(k, carry):
            body(k)
            return carry

        lax.fori_loop(0, count, step, 0)

    load_up = pltpu.make_async_copy(up_ref, xin.at[pl.ds(0, ROWS)], local_sem.at[0])
    load_dn = pltpu.make_async_copy(down_ref, xin.at[pl.ds(ROWS, ROWS)], local_sem.at[1])
    load_wg = pltpu.make_async_copy(wg_ref, wg.at[0], local_sem.at[2])
    load_wu = pltpu.make_async_copy(wu_ref, wu.at[0], local_sem.at[3])
    load_wd = pltpu.make_async_copy(wd_ref.at[:, half_mine], wd.at[0], local_sem.at[4])
    load_gain = pltpu.make_async_copy(gain_ref, gain_vm, local_sem.at[5])
    load_router = pltpu.make_async_copy(router_ref, router_vm, local_sem.at[6])
    load_ru = pltpu.make_async_copy(routes_up, routes_vm.at[0], local_sem.at[7])
    load_rd = pltpu.make_async_copy(routes_down, routes_vm.at[1], local_sem.at[8])
    load_up.start()
    load_dn.start()
    load_ru.start()
    load_rd.start()
    load_gain.start()
    load_router.start()
    barrier = pltpu.get_barrier_semaphore()
    for to in (xn, zn, xc, core, above, below):
        pl.semaphore_signal(barrier, inc=1, device_id=to, device_id_type=MESH)

    @pl.when(low | high)
    def _():
        for to in (across, next_row, last_row):
            pl.semaphore_signal(barrier, inc=1, device_id=to, device_id_type=MESH)

    load_wg.start()
    load_wu.start()
    load_wd.start()

    token_r = lax.broadcasted_iota(jnp.int32, (128, 128), 0)
    token_c = lax.broadcasted_iota(jnp.int32, (128, 128), 1)
    load_ru.wait()
    load_rd.wait()
    wide_up = dot(routes_vm[0].astype(F32), jnp.where(token_r[:64] == token_c[:64], 1.0, 0.0))
    wide_dn = dot(routes_vm[1].astype(F32), jnp.where(token_r[:64] + 64 == token_c[:64], 1.0, 0.0))
    chosen = jnp.broadcast_to((wide_up + wide_dn).astype(jnp.int32), (128, 128))
    mine = (chosen == expert).astype(F32)
    before = ((token_r < token_c) & (token_r // 64 == token_c // 64)).astype(F32)
    ahead = dot(mine.astype(BF16), before.astype(BF16))
    inside = (token_c % 64).astype(F32)
    stream = (token_c // 64 * 32).astype(F32)
    target = stream + jnp.where(mine > 0.5, ahead, 64.0 + inside - ahead)
    hit = (token_r.astype(F32) == target).astype(F32)
    place[...] = hit.astype(BF16)
    place_t[...] = hit.T.astype(BF16)

    load_up.wait()
    load_dn.wait()

    def squares(k, total):
        part = xin[:, cols(k)].astype(F32)
        return total + jnp.sum(part * part, axis=1, keepdims=True)

    total = lax.fori_loop(0, NK, squares, jnp.zeros((128, 1), F32))
    inverse = lax.rsqrt(total * (1.0 / D) + EPSILON)
    weight[...] = jnp.broadcast_to(inverse, (128, 128))

    def normed(k):
        gain = gain_vm[:, cols(k)].astype(F32)
        return (xin[:, cols(k)].astype(F32) * weight[:, 0:1] * gain).astype(BF16)

    load_gain.wait()
    load_router.wait()
    pl.semaphore_wait(barrier, jnp.where(low | high, 9, 6))

    def first(k):
        moved = dot(place[...], normed(k)).astype(BF16)
        xb[OWN, :, cols(k)] = moved[:ROWS]
        fb[:, cols(k)] = moved[ROWS:]
        cross(k).start()
        own_x(k).start()
        own_z(k).start()

    loop(NK, first)
    wg_core.start()
    wu_core.start()
    wd_core.start()

    def affinity(k, carry):
        zero, one = carry
        part = normed(k).astype(F32)
        near = router_vm[:, cols(k)].astype(F32)
        zero = zero + jnp.sum(part * near[0:1], axis=1, keepdims=True)
        one = one + jnp.sum(part * near[1:2], axis=1, keepdims=True)
        return zero, one

    empty = jnp.zeros((128, 1), F32)
    zero, one = lax.fori_loop(0, NK, affinity, (empty, empty))
    named = jnp.where(token_r == token_c, chosen, 0).astype(F32)
    named = jnp.sum(named, axis=1, keepdims=True)
    logit = jnp.where(named > 0.5, one, zero)
    weight[...] = jnp.broadcast_to(ROUTE_SCALE * jax.nn.sigmoid(logit), (128, 128))

    load_wg.wait()
    load_wu.wait()
    load_wd.wait()
    wg_core.wait_recv()
    wu_core.wait_recv()

    def hidden_step(pair, k):
        rows = xb[pl.ds(2 * pair, 2), :, cols(k)].reshape(2 * ROWS, KC)
        gate = dot(rows, jnp.concatenate([wg[0, cols(k)], wg[1, cols(k)]], axis=1))
        up = dot(rows, jnp.concatenate([wu[0, cols(k)], wu[1, cols(k)]], axis=1))
        first_one = k == 0
        acc[:, 0:256] = jnp.where(first_one, 0.0, acc[:, 0:256]) + gate
        acc[:, 256:512] = jnp.where(first_one, 0.0, acc[:, 256:512]) + up

    def hidden_end(pair):
        act = jax.nn.silu(acc[:, 0:256]) * acc[:, 256:512]
        actm[pl.ds(pair * 2 * ROWS, 2 * ROWS)] = act.astype(BF16)
        act_z(pair).start()

    acc[...] = jnp.zeros_like(acc)

    def second(k):
        cross(k).wait_recv()
        ent_x(k).start()
        ent_z(k).start()
        own_z(k).wait_recv()
        fwd_own(k).start()
        hidden_step(0, k)

    loop(NK, second)
    wd_z.start()
    hidden_end(0)

    def third(k):
        ent_z(k).wait_recv()

        @pl.when(k < KX)
        def _():
            fwd_ent_x(k).start()

        hidden_step(1, k)

    loop(NK, third)
    hidden_end(1)

    def fourth(k):
        own_x(k).wait_recv()
        fwd_own(k).wait_recv()
        hidden_step(2, k)

    loop(NK, fourth)
    hidden_end(2)

    def relay(k):
        ent_x(k).wait_recv()

        @pl.when(k >= KX)
        def _():
            fwd_ent_z(k).start()

    loop(NK, relay)
    wd_z.wait_recv()
    wd_relay.start()
    wd_core.wait_recv()

    def back(pair, j):
        at = pl.ds(pl.multiple_of(j * JC, JC), JC)
        base = pair * 2 * ROWS
        far = jnp.concatenate([actz[base + ROWS:base + 2 * ROWS], actz[base:base + ROWS]], axis=0)
        left = jnp.concatenate([actm[base:base + 2 * ROWS], far], axis=1)
        return dot(left, wd[:, :, at].reshape(4 * HID, JC))

    def back_o(j):
        sx[j, 0:128] = back(2, j).astype(BF16)
        ret_xo(j).start()

    def back_e(j):
        sx[j, 128:256] = back(3, j).astype(BF16)
        ret_xe(j).start()

    def fifth(k):
        fwd_ent_x(k).wait_recv()
        hidden_step(3, k)

    loop(KX, fifth)
    act_z(2).wait_recv()
    wd_relay.wait_recv()
    loop(3, back_o)

    def sixth(k):
        fwd_ent_z(k + KX).wait_recv()
        hidden_step(3, k + KX)

    loop(NK - KX, sixth)
    hidden_end(3)

    act_z(3).wait_recv()

    def pieces(j):
        @pl.when(j >= 3)
        def _():
            back_o(j)

        back_e(j)

    loop(NJ, pieces)
    act_z(0).wait_recv()
    act_z(1).wait_recv()

    def drain(k):
        own_x(k).wait_send()
        own_z(k).wait_send()
        cross(k).wait_send()
        ent_x(k).wait_send()
        ent_z(k).wait_send()
        fwd_own(k).wait_send()
        fwd_ent_x(k).wait_send()

    loop(NK, drain)
    for copy in (wd_z, wd_relay, wd_core, wg_core, wu_core, act_z(0), act_z(1), act_z(2), act_z(3)):
        copy.wait_send()

    def sums(j):
        near = back(0, j)
        ret_xo(j).wait_recv()
        near = near + rx[j, 0:128].astype(F32)
        sz[j, 0:ROWS] = near[ROWS:].astype(BF16)
        ret_zo(j).start()
        fa[j, 0:ROWS] = near[:ROWS].astype(BF16)
        far = back(1, j)
        ret_xe(j).wait_recv()
        far = far + rx[j, 128:256].astype(F32)
        sz[j, ROWS:128] = far[ROWS:].astype(BF16)
        ret_zc(j).start()
        sc[j] = far[:ROWS].astype(BF16)
        ret_c(j).start()

    def finish(j, part, held):
        mixed = dot(place_t[...], held[j])
        out = xin[:, out_cols(j, part)].astype(F32) + weight[:, 0:1] * mixed
        outb[j, part] = out.astype(BF16)
        if part == 1:
            send_up(j, 1).start()
            send_dn(j, 1).start()
            return

        @pl.when(high)
        def _():
            detour_up(j).start()

        @pl.when(~high)
        def _():
            send_up(j, 0).start()

        @pl.when(low)
        def _():
            detour_dn(j).start()

        @pl.when(~low)
        def _():
            send_dn(j, 0).start()

    def onward(j):
        @pl.when(low)
        def _():
            detour_up(j).wait_recv()
            onward_up(j).start()

        @pl.when(high)
        def _():
            detour_dn(j).wait_recv()
            onward_dn(j).start()

    def final(j):
        ret_c(j).wait_recv()
        finish(j, 0, fa)
        ret_zo(j).wait_recv()
        ret_zc(j).wait_recv()
        finish(j, 1, fz)

    def tail(i):
        @pl.when(i < NJ)
        def _():
            sums(i)

        @pl.when((i >= 2) & (i < NJ + 2))
        def _():
            final(i - 2)

        @pl.when(i >= 3)
        def _():
            onward(i - 3)

    loop(NJ + 3, tail)

    def last(j):
        ret_xo(j).wait_send()
        ret_xe(j).wait_send()
        ret_zo(j).wait_send()
        ret_zc(j).wait_send()
        ret_c(j).wait_send()
        send_up(j, 1).wait_send()
        send_dn(j, 1).wait_send()

        @pl.when(high)
        def _():
            detour_up(j).wait_send()
            onward_dn(j).wait_send()

        @pl.when(~high)
        def _():
            send_up(j, 0).wait_send()

        @pl.when(low)
        def _():
            detour_dn(j).wait_send()
            onward_up(j).wait_send()

        @pl.when(~low)
        def _():
            send_dn(j, 0).wait_send()

        for part in range(2):
            send_up(j, part).wait_recv()
            send_dn(j, part).wait_recv()

    loop(NJ, last)


def local(stream_up, stream_down, norm_gain, router, w_gate, w_up, w_down, routes_up, routes_down):
    any_spec = pl.BlockSpec(memory_space=pl.ANY)
    out = jax.ShapeDtypeStruct((ROWS, D), BF16)
    rising, falling = pl.pallas_call(
        kernel,
        out_shape=(out, out),
        in_specs=[any_spec] * 9,
        out_specs=(any_spec, any_spec),
        scratch_shapes=[
            pltpu.VMEM((128, D), BF16),
            pltpu.VMEM((1, D), BF16),
            pltpu.VMEM((2, D), BF16),
            pltpu.VMEM((2, 1, ROWS), jnp.int32),
            pltpu.VMEM((8, ROWS, D), BF16),
            pltpu.VMEM((ROWS, D), BF16),
            pltpu.VMEM((2, D, HID), BF16),
            pltpu.VMEM((2, D, HID), BF16),
            pltpu.VMEM((4, HID, HALF), BF16),
            pltpu.VMEM((8 * ROWS, 2 * HID), BF16),
            pltpu.VMEM((8 * ROWS, 2 * HID), BF16),
            pltpu.VMEM((2 * ROWS, 4 * HID), F32),
            pltpu.VMEM((NJ, 4 * ROWS, JC), BF16),
            pltpu.VMEM((NJ, 4 * ROWS, JC), BF16),
            pltpu.VMEM((NJ, 2 * ROWS, JC), BF16),
            pltpu.VMEM((NJ, ROWS, JC), BF16),
            pltpu.VMEM((NJ, 2 * ROWS, JC), BF16),
            pltpu.VMEM((NJ, 2 * ROWS, JC), BF16),
            pltpu.VMEM((NJ, 2, 2 * ROWS, JC), BF16),
            pltpu.VMEM((NJ, ROWS, JC), BF16),
            pltpu.VMEM((NJ, ROWS, JC), BF16),
            pltpu.VMEM((128, 128), BF16),
            pltpu.VMEM((128, 128), BF16),
            pltpu.VMEM((128, 128), F32),
            pltpu.SemaphoreType.DMA((9,)),
            pltpu.SemaphoreType.DMA((N_SEM,)),
            pltpu.SemaphoreType.DMA((N_SEM,)),
        ],
        compiler_params=pltpu.CompilerParams(
            collective_id=0, has_side_effects=True, vmem_limit_bytes=60 * 2**20
        ),
        name="relay",
    )(
        stream_up[0], stream_down[0], norm_gain, router[0].T, w_gate[0], w_up[0], w_down[0],
        routes_up.reshape(1, ROWS), routes_down.reshape(1, ROWS),
    )
    return rising[None], falling[None]


def solution(mesh):
    placed = (
        P("pp", "ep", None),
        P("pp", "ep", None),
        P("pp", None),
        P("pp", None, None),
        P("pp", None, "ep"),
        P("pp", None, "ep"),
        P("pp", "ep", None),
        P(None, "pp", "ep", None),
        P(None, "pp", "ep", None),
    )
    return jax.shard_map(
        local,
        mesh=mesh,
        in_specs=placed,
        out_specs=(P("pp", "ep", None), P("pp", "ep", None)),
        check_vma=False,
    )
```

```python
import jax
import jax.numpy as jnp
from jax import lax
from jax.experimental import pallas as pl
from jax.experimental.pallas import tpu as pltpu
from jax.sharding import PartitionSpec as P

MESH = pl.DeviceIdType.MESH
F32 = jnp.float32
BF16 = jnp.bfloat16
EPSILON = 1e-06
ROUTE_SCALE = 2.5

D = 7168
ROWS = 64
HID = 128
HALF = D // 2
KC = 1024
NK = D // KC
JC = 512
NJ = HALF // JC
NB = NJ - 2
NR = NB + 4
KX = 3

OWN, Z_OWN, ENT, Z_ENT, X_OWN, D_OWN, X_ENT, D_ENT = range(8)

OWN_X, OWN_Z, CROSS, ENT_X, ENT_Z, FWD_OWN, FWD_ENT = range(0, 7 * NK, NK)
W_BASE = 7 * NK
WD_Z, WD_RELAY, WD_CORE, WG_CORE, WU_CORE = range(W_BASE, W_BASE + 5)
ACT_Z = W_BASE + 5
R_BASE = ACT_Z + 4
RET_XO, RET_XE, RET_ZO, RET_ZC, RET_C = range(R_BASE, R_BASE + 5 * NR, NR)
OUT_UP = R_BASE + 5 * NR
OUT_DN = OUT_UP + 4 * NJ
RELAY = OUT_DN + 4 * NJ
ONWARD = RELAY + 4 * NJ
PERM_UP = ONWARD + 4 * NJ
PERM_DN = PERM_UP + 1
N_SEM = PERM_DN + 1


def dot(a, b):
    return jnp.dot(a, b, preferred_element_type=F32)


def kernel(
    up_ref, down_ref, gain_ref, router_ref, wg_ref, wu_ref, wd_ref, routes_up, routes_down,
    out_up, out_dn, out_perm,
    xin, xs, gain_vm, router_vm, routes_vm, xb, fb, wg, wu, wd, actm, actz, acc, sx, rx, sz, sc, fc, fz, outb,
    via, place, perm, weight, local_sem, send_sem, recv_sem, ready,
):
    pp = lax.axis_index("pp")
    ep = lax.axis_index("ep")
    n_pp = lax.axis_size("pp")
    xi = ep // 4
    zi = (ep // 2) % 2
    ci = ep % 2

    def device(x, z, c):
        return (pp, x * 4 + z * 2 + c)

    xn = device(xi + 1 - 2 * (xi % 2), zi, ci)
    zn = device(xi, 1 - zi, ci)
    xc = device(3 - xi, zi, ci)
    xc_zn = device(3 - xi, 1 - zi, ci)
    core = device(xi, zi, 1 - ci)
    above = (lax.rem(pp + 1, n_pp), ep)
    below = (lax.rem(pp + n_pp - 1, n_pp), ep)
    expert = xi // 2

    yi = pp % 4
    falls = yi == 0

    def section(step):
        return (lax.rem(pp + n_pp + step, n_pp), ep)

    my_half = zi * HALF
    other_half = (1 - zi) * HALF

    def remote(src, dst, index, to):
        return pltpu.make_async_remote_copy(
            src_ref=src,
            dst_ref=dst,
            send_sem=send_sem.at[index],
            recv_sem=recv_sem.at[index],
            device_id=to,
            device_id_type=MESH,
        )

    def cols(k):
        return pl.ds(pl.multiple_of(k * KC, KC), KC)

    def block(slot, k):
        return xb.at[slot, :, cols(k)]

    def own_x(k):
        return remote(block(OWN, k), block(X_OWN, k), OWN_X + k, xn)

    def own_z(k):
        return remote(block(OWN, k), block(Z_OWN, k), OWN_Z + k, zn)

    def cross(k):
        return remote(fb.at[:, cols(k)], block(ENT, k), CROSS + k, xc)

    def ent_x(k):
        return remote(block(ENT, k), block(X_ENT, k), ENT_X + k, xn)

    def ent_z(k):
        return remote(block(ENT, k), block(Z_ENT, k), ENT_Z + k, zn)

    def fwd_own(k):
        return remote(block(Z_OWN, k), block(D_OWN, k), FWD_OWN + k, xn)

    def fwd_ent_x(k):
        return remote(block(Z_ENT, k), block(D_ENT, k), FWD_ENT + k, xn)

    def fwd_ent_z(k):
        return remote(block(X_ENT, k), block(D_ENT, k), FWD_ENT + k, zn)

    half_mine = pl.ds(pl.multiple_of(my_half, HALF), HALF)
    half_other = pl.ds(pl.multiple_of(other_half, HALF), HALF)
    wd_z = remote(wd_ref.at[:, half_other], wd.at[2], WD_Z, zn)
    wd_relay = remote(wd.at[2], wd.at[3], WD_RELAY, core)
    wd_core = remote(wd_ref.at[:, half_mine], wd.at[1], WD_CORE, core)
    wg_core = remote(wg_ref, wg.at[1], WG_CORE, core)
    wu_core = remote(wu_ref, wu.at[1], WU_CORE, core)

    def act_z(pair):
        rows = pl.ds(pair * 2 * ROWS, 2 * ROWS)
        return remote(actm.at[rows], actz.at[rows], ACT_Z + pair, zn)

    def piece(j, streams=(0, 1)):
        p = j + 2 if streams == (1,) else j
        return p, j, pl.multiple_of(j * JC, JC), streams

    def span(streams, base, rows):
        return pl.ds(base + streams[0] * rows, len(streams) * rows)

    def ret_xo(p, j, at, streams):
        part = (span(streams, 0, ROWS), pl.ds(at, JC))
        return remote(sx.at[part], rx.at[part], RET_XO + p, xn)

    def ret_xe(p, j, at, streams):
        part = (span(streams, 128, ROWS), pl.ds(at, JC))
        return remote(sx.at[part], rx.at[part], RET_XE + p, xn)

    def ret_zo(p, j, at, streams):
        part = (span(streams, 0, 32), pl.ds(at, JC))
        return remote(sz.at[part], fz.at[part], RET_ZO + p, zn)

    def ret_zc(p, j, at, streams):
        part = (span(streams, ROWS, 32), pl.ds(at, JC))
        return remote(sz.at[part], fz.at[part], RET_ZC + p, xc_zn)

    def ret_c(p, j, at, streams):
        part = (span(streams, 0, 32), pl.ds(at, JC))
        return remote(sc.at[part], fc.at[part], RET_C + p, xc)

    def out_cols(at, n, half):
        start = jnp.where(half == 0, my_half, other_half) + at
        return pl.ds(pl.multiple_of(start, 128), n)

    def moved(src, dst, send, recv, to):
        return pltpu.make_async_remote_copy(
            src_ref=src,
            dst_ref=dst,
            send_sem=send_sem.at[send],
            recv_sem=recv_sem.at[recv],
            device_id=to,
            device_id_type=MESH,
        )

    def out_src(q, stream, at):
        return outb.at[q % 2, pl.ds(q // 2 * ROWS + stream * 32, 32), pl.ds(at, JC)]

    def row_at(q):
        row = q // 2 * 32
        return pl.ds(row if isinstance(q, int) else pl.multiple_of(row, 32), 32)

    def out_dst(ref, q, at):
        return ref.at[row_at(q), out_cols(at, JC, q % 2)]

    def send_up(stream, j, at, q):
        index = OUT_UP + 4 * j + q
        return moved(out_src(q, stream, at), out_dst(out_up, q, at), index, index, above)

    def send_dn(stream, j, at, q):
        index = OUT_DN + 4 * j + q
        return moved(out_src(q, stream, at), out_dst(out_dn, q, at), index, index, below)

    def turn(j, q):
        return jnp.where((j >= NB) & (q >= 2), 3, lax.rem(j + q, 4))

    def via_at(q, at):
        return via.at[q % 2, row_at(q), pl.ds(at, JC)]

    def detour(j, at, q):
        index = RELAY + 4 * j + q
        step = 3 - turn(j, q)
        to = section(jnp.where(falls, step, -step))
        return moved(out_src(q, 0, at), via_at(q, at), index, index, to)

    def arrived(j, at, q):
        index = RELAY + 4 * j + q
        return moved(via_at(q, at), via_at(q, at), index, index, above)

    def onward_up(j, at, q):
        dst = out_dst(out_up, q, at)
        index = 4 * j + q
        return moved(via_at(q, at), dst, ONWARD + index, OUT_UP + index, section(4 - yi))

    def onward_dn(j, at, q):
        dst = out_dst(out_dn, q, at)
        index = 4 * j + q
        return moved(via_at(q, at), dst, ONWARD + index, OUT_DN + index, section(-1 - yi))

    def perm_up(stream):
        return moved(perm.at[stream], out_perm.at[0], PERM_UP, PERM_UP, above)

    def perm_dn(stream):
        return moved(perm.at[stream], out_perm.at[1], PERM_DN, PERM_DN, below)

    def by_stream(act_0, act_1):
        @pl.when(falls)
        def _():
            act_0(1)
            act_1(0)

        @pl.when(~falls)
        def _():
            act_0(0)
            act_1(1)

    def loop(count, body):
        def step(k, carry):
            body(k)
            return carry

        lax.fori_loop(0, count, step, 0)

    def load_x(s, src):
        return pltpu.make_async_copy(src, xin.at[pl.ds(s * ROWS, ROWS)], local_sem.at[s])

    def load_routes(s, src):
        return pltpu.make_async_copy(src, routes_vm.at[s], local_sem.at[7 + s])

    def load_streams(first, second, routes_first, routes_second):
        load_x(0, first).start()
        load_x(1, second).start()
        load_routes(0, routes_first).start()
        load_routes(1, routes_second).start()

    @pl.when(falls)
    def _():
        load_streams(down_ref, up_ref, routes_down, routes_up)

    @pl.when(~falls)
    def _():
        load_streams(up_ref, down_ref, routes_up, routes_down)

    load_wg = pltpu.make_async_copy(wg_ref, wg.at[0], local_sem.at[2])
    load_wu = pltpu.make_async_copy(wu_ref, wu.at[0], local_sem.at[3])
    load_wd = pltpu.make_async_copy(wd_ref.at[:, half_mine], wd.at[0], local_sem.at[4])
    load_gain = pltpu.make_async_copy(gain_ref, gain_vm, local_sem.at[5])
    load_router = pltpu.make_async_copy(router_ref, router_vm, local_sem.at[6])
    load_gain.start()
    load_router.start()
    barrier = pltpu.get_barrier_semaphore()
    near = (xn, zn, xc, xc_zn, core)
    steps = (-4, -3, -2, -1, 1, 2, 3, 4)
    lower = sum((section(step)[0] < pp).astype(jnp.int32) for step in steps)
    for to in near:
        pl.semaphore_signal(barrier, inc=1, device_id=to, device_id_type=MESH)
    for step in steps:
        to = section(step)

        @pl.when(to[0] > pp)
        def _():
            pl.semaphore_signal(barrier, inc=1, device_id=to, device_id_type=MESH)

    load_wg.start()
    load_wu.start()
    load_wd.start()

    token_r = lax.broadcasted_iota(jnp.int32, (128, 128), 0)
    token_c = lax.broadcasted_iota(jnp.int32, (128, 128), 1)
    load_routes(0, routes_up).wait()
    load_routes(1, routes_down).wait()
    wide_0 = dot(routes_vm[0].astype(F32), jnp.where(token_r[:64] == token_c[:64], 1.0, 0.0))
    wide_1 = dot(routes_vm[1].astype(F32), jnp.where(token_r[:64] + 64 == token_c[:64], 1.0, 0.0))
    chosen = jnp.broadcast_to((wide_0 + wide_1).astype(jnp.int32), (128, 128))
    mine = (chosen == expert).astype(F32)
    before = ((token_r < token_c) & (token_r // 64 == token_c // 64)).astype(F32)
    ahead = dot(mine.astype(BF16), before.astype(BF16))
    inside = (token_c % 64).astype(F32)
    stream = (token_c // 64 * 32).astype(F32)
    target = stream + jnp.where(mine > 0.5, ahead, 64.0 + inside - ahead)
    hit = (token_r.astype(F32) == target).astype(F32)
    place[...] = hit.astype(BF16)
    back_to = stream * 2.0 + jnp.where(mine > 0.5, ahead, 32.0 + inside - ahead)
    back_hit = (token_r.astype(F32) == back_to).astype(F32).T.astype(BF16)
    perm[...] = jnp.zeros_like(perm)
    perm[0, :, 0:ROWS] = back_hit[:ROWS, :ROWS]
    perm[1, :, 0:ROWS] = back_hit[ROWS:, ROWS:]

    load_x(0, up_ref).wait()
    load_x(1, down_ref).wait()

    def squares(k, total):
        part = xin[:, cols(k)].astype(F32)
        part = part * part
        for c in range(KC // 128):
            total = total + part[:, c * 128:(c + 1) * 128]
        return total

    total = lax.fori_loop(0, NK, squares, jnp.zeros((128, 128), F32))
    total = jnp.sum(total, axis=1, keepdims=True)
    inverse = lax.rsqrt(total * (1.0 / D) + EPSILON)
    weight[...] = jnp.broadcast_to(inverse, (128, 128))

    def normed(k):
        gain = gain_vm[:, cols(k)].astype(F32)
        return (xin[:, cols(k)].astype(F32) * weight[:, 0:1] * gain).astype(BF16)

    load_gain.wait()
    load_router.wait()
    pl.semaphore_wait(barrier, len(near) + lower)
    for step in steps:
        to = section(step)

        @pl.when(to[0] < pp)
        def _():
            pl.semaphore_signal(ready, inc=1, device_id=to, device_id_type=MESH)


    def first(k):
        moved = dot(place[...], normed(k)).astype(BF16)
        xb[OWN, :, cols(k)] = moved[:ROWS]
        fb[:, cols(k)] = moved[ROWS:]
        cross(k).start()
        own_x(k).start()
        own_z(k).start()

    loop(NK, first)
    wg_core.start()
    wu_core.start()
    wd_core.start()

    def affinity(k, carry):
        own, foreign = carry
        zero = router_vm[0:1, cols(k)].astype(F32)
        one = router_vm[1:2, cols(k)].astype(F32)
        near, far = jnp.where(expert == 0, zero, one), jnp.where(expert == 0, one, zero)
        own = own + jnp.sum(xb[OWN, :, cols(k)].astype(F32) * near, axis=1, keepdims=True)
        foreign = foreign + jnp.sum(fb[:, cols(k)].astype(F32) * far, axis=1, keepdims=True)
        xs[:, cols(k)] = dot(place[...], xin[:, cols(k)]).astype(BF16)
        return own, foreign

    empty = jnp.zeros((ROWS, 1), F32)
    own, foreign = lax.fori_loop(0, NK, affinity, (empty, empty))
    weight[0:ROWS] = jnp.broadcast_to(ROUTE_SCALE * jax.nn.sigmoid(own), (ROWS, 128))
    weight[ROWS:] = jnp.broadcast_to(ROUTE_SCALE * jax.nn.sigmoid(foreign), (ROWS, 128))

    load_wg.wait()
    load_wu.wait()
    load_wd.wait()
    wg_core.wait_recv()
    wu_core.wait_recv()

    def hidden_step(pair, k):
        rows = xb[pl.ds(2 * pair, 2), :, cols(k)].reshape(2 * ROWS, KC)
        gate = dot(rows, jnp.concatenate([wg[0, cols(k)], wg[1, cols(k)]], axis=1))
        up = dot(rows, jnp.concatenate([wu[0, cols(k)], wu[1, cols(k)]], axis=1))
        first_one = k == 0
        acc[:, 0:256] = jnp.where(first_one, 0.0, acc[:, 0:256]) + gate
        acc[:, 256:512] = jnp.where(first_one, 0.0, acc[:, 256:512]) + up

    def hidden_end(pair):
        act = jax.nn.silu(acc[:, 0:256]) * acc[:, 256:512]
        act = act.astype(BF16)
        for n, row in enumerate((0, ROWS, 32, ROWS + 32)):
            actm[pl.ds(pair * 2 * ROWS + n * 32, 32)] = act[row:row + 32]
        act_z(pair).start()

    acc[...] = jnp.zeros_like(acc)

    def second(k):
        cross(k).wait_recv()
        ent_x(k).start()
        ent_z(k).start()
        own_z(k).wait_recv()
        fwd_own(k).start()
        hidden_step(0, k)

    loop(NK, second)
    wd_z.start()

    @pl.when(lower < len(steps))
    def _():
        pl.semaphore_wait(ready, len(steps) - lower)

    by_stream(lambda s: perm_up(s).start(), lambda s: perm_dn(s).start())
    hidden_end(0)

    def third(k):
        ent_z(k).wait_recv()

        @pl.when(k < KX)
        def _():
            fwd_ent_x(k).start()

        hidden_step(1, k)

    loop(NK, third)
    hidden_end(1)

    def fourth(k):
        own_x(k).wait_recv()
        fwd_own(k).wait_recv()
        hidden_step(2, k)

    loop(NK, fourth)
    hidden_end(2)

    def relay(k):
        ent_x(k).wait_recv()

        @pl.when(k >= KX)
        def _():
            fwd_ent_z(k).start()

    loop(NK, relay)
    wd_z.wait_recv()
    wd_relay.start()
    wd_core.wait_recv()

    def back(pair, at, streams):
        base = pair * 2 * ROWS
        far = []
        for s in streams:
            first = base + s * ROWS
            far += [actz[first + 32:first + 64], actz[first:first + 32]]
        first = base + streams[0] * ROWS
        near = actm[first:first + len(streams) * ROWS]
        left = jnp.concatenate([near, jnp.concatenate(far, axis=0)], axis=1)
        return dot(left, wd[:, :, pl.ds(at, JC)].reshape(4 * HID, JC))

    def back_o(p, j, at, streams):
        sx[span(streams, 0, ROWS), pl.ds(at, JC)] = back(2, at, streams).astype(BF16)
        ret_xo(p, j, at, streams).start()

    def back_e(p, j, at, streams):
        sx[span(streams, 128, ROWS), pl.ds(at, JC)] = back(3, at, streams).astype(BF16)
        ret_xe(p, j, at, streams).start()

    def finish(j, at, q, total, streams):
        rows = span(streams, q // 2 * ROWS, 32)
        out = xs[rows, out_cols(at, JC, q % 2)].astype(F32) + weight[rows, 0:1] * total
        outb[q % 2, rows, pl.ds(at, JC)] = out.astype(BF16)
        if 0 in streams:
            straight = (turn(j, q) == 3) | (yi == 1) | (yi == 2)

            @pl.when(straight & falls)
            def _():
                send_dn(0, j, at, q).start()

            @pl.when(straight & ~falls)
            def _():
                send_up(0, j, at, q).start()

            @pl.when(~straight)
            def _():
                detour(j, at, q).start()

        if 1 in streams:

            @pl.when(falls)
            def _():
                send_up(1, j, at, q).start()

            @pl.when(~falls)
            def _():
                send_dn(1, j, at, q).start()

    def parted(total):
        blocks = [[total[r:r + 32] for r in range(b, total.shape[0], ROWS)] for b in (0, 32)]
        return [jnp.concatenate(b, axis=0) for b in blocks]

    def sums_o(p, j, at, streams):
        total = back(0, at, streams)
        ret_xo(p, j, at, streams).wait_recv()
        total = total + rx[span(streams, 0, ROWS), pl.ds(at, JC)].astype(F32)
        mine_o, other = parted(total)
        sz[span(streams, 0, 32), pl.ds(at, JC)] = other.astype(BF16)
        ret_zo(p, j, at, streams).start()
        finish(j, at, 0, mine_o, streams)

    def sums_e(p, j, at, streams):
        total = back(1, at, streams)
        ret_xe(p, j, at, streams).wait_recv()
        total = total + rx[span(streams, 128, ROWS), pl.ds(at, JC)].astype(F32)
        mine_e, other = parted(total)
        sz[span(streams, ROWS, 32), pl.ds(at, JC)] = other.astype(BF16)
        ret_zc(p, j, at, streams).start()
        sc[span(streams, 0, 32), pl.ds(at, JC)] = mine_e.astype(BF16)
        ret_c(p, j, at, streams).start()

    def final_o(p, j, at, streams):
        ret_zo(p, j, at, streams).wait_recv()
        finish(j, at, 1, fz[span(streams, 0, 32), pl.ds(at, JC)].astype(F32), streams)

    def final_e(p, j, at, streams):
        ret_c(p, j, at, streams).wait_recv()
        finish(j, at, 2, fc[span(streams, 0, 32), pl.ds(at, JC)].astype(F32), streams)
        ret_zc(p, j, at, streams).wait_recv()
        finish(j, at, 3, fz[span(streams, ROWS, 32), pl.ds(at, JC)].astype(F32), streams)

    def relays(j):
        return lax.rem(yi + 4 * NJ - j, 4), lax.rem(3 - yi + 4 * NJ - j, 4)

    def pass_on(kind, p, j, at, streams):
        up, dn = relays(j)

        @pl.when((yi != 3) & (up // 2 == kind))
        def _():
            arrived(j, at, up).wait_recv()
            onward_up(j, at, up).start()

        @pl.when((yi != 0) & (dn // 2 == kind))
        def _():
            arrived(j, at, dn).wait_recv()
            onward_dn(j, at, dn).start()

    def fifth(k):
        fwd_ent_x(k).wait_recv()
        hidden_step(3, k)

    act_z(2).wait_recv()
    wd_relay.wait_recv()
    loop(2, lambda j: back_o(*piece(j)))
    loop(KX, fifth)
    loop(NB - 2, lambda j: back_o(*piece(j + 2)))
    act_z(0).wait_recv()
    act_z(1).wait_recv()

    def sixth(k):
        fwd_ent_z(k + KX).wait_recv()
        hidden_step(3, k + KX)

    loop(NK - KX - 1, sixth)
    sums_o(*piece(0))
    sixth(NK - KX - 1)
    hidden_end(3)
    sums_o(*piece(1))
    sums_o(*piece(2))

    def drain(k):
        own_x(k).wait_send()
        own_z(k).wait_send()
        cross(k).wait_send()
        ent_x(k).wait_send()
        ent_z(k).wait_send()
        fwd_own(k).wait_send()
        fwd_ent_x(k).wait_send()

    loop(NK, drain)
    act_z(3).wait_recv()
    first = [piece(NB, (0,)), piece(NB + 1, (0,))]
    second = [piece(NB, (1,)), piece(NB + 1, (1,))]
    loop(2, lambda j: back_e(*piece(j)))
    for part in first:
        back_o(*part)

    def step(i):
        @pl.when(i + 2 < NB)
        def _():
            back_e(*piece(i + 2))

        @pl.when(i == NB - 3)
        def _():
            for part in first:
                back_e(*part)

        @pl.when(i == NB - 2)
        def _():
            for part in second:
                back_e(*part)
            for part in second:
                back_o(*part)
            for part in first:
                sums_o(*part)

        @pl.when(i + 3 < NB)
        def _():
            sums_o(*piece(i + 3))

        final_o(*piece(i))
        sums_e(*piece(i))

        @pl.when(i >= 1)
        def _():
            final_e(*piece(i - 1))

        @pl.when(i >= 2)
        def _():
            pass_on(0, *piece(i - 2))

        @pl.when(i >= 3)
        def _():
            pass_on(1, *piece(i - 3))

    loop(NB, step)
    for part in first:
        final_o(*part)
    sums_e(*first[0])
    final_e(*piece(NB - 1))
    sums_e(*first[1])
    pass_on(0, *piece(NB - 2))
    pass_on(0, *piece(NB - 1))
    pass_on(1, *piece(NB - 3))
    pass_on(1, *piece(NB - 2))
    pass_on(0, *first[0])
    pass_on(0, *first[1])
    sums_e(*second[0])
    final_e(*first[0])
    sums_e(*second[1])
    final_e(*first[1])
    pass_on(1, *piece(NB - 1))
    sums_o(*second[0])
    sums_o(*second[1])
    final_e(*second[0])
    final_o(*second[0])
    final_e(*second[1])
    final_o(*second[1])

    for copy in (wd_z, wd_relay, wd_core, wg_core, wu_core, act_z(0), act_z(1), act_z(2), act_z(3)):
        copy.wait_send()
    by_stream(lambda s: perm_up(s).wait(), lambda s: perm_dn(s).wait())

    def sent(p, j, at, streams):
        ret_xo(p, j, at, streams).wait_send()
        ret_xe(p, j, at, streams).wait_send()
        ret_zo(p, j, at, streams).wait_send()
        ret_zc(p, j, at, streams).wait_send()
        ret_c(p, j, at, streams).wait_send()

    def last(p, j, at, streams):
        up, dn = relays(j)

        @pl.when((yi != 3) & ((j < NB) | (up < 2)))
        def _():
            onward_up(j, at, up).wait_send()

        @pl.when((yi != 0) & ((j < NB) | (dn < 2)))
        def _():
            onward_dn(j, at, dn).wait_send()

        for q in range(4):
            straight = (turn(j, q) == 3) | (yi == 1) | (yi == 2)

            @pl.when(falls)
            def _():
                send_up(1, j, at, q).wait_send()

            @pl.when(~falls)
            def _():
                send_dn(1, j, at, q).wait_send()

            @pl.when(straight & falls)
            def _():
                send_dn(0, j, at, q).wait_send()

            @pl.when(straight & ~falls)
            def _():
                send_up(0, j, at, q).wait_send()

            @pl.when(~straight)
            def _():
                detour(j, at, q).wait_send()

            send_up(0, j, at, q).wait_recv()
            send_dn(0, j, at, q).wait_recv()

    loop(NB, lambda j: sent(*piece(j)))
    for part in first + second:
        sent(*part)
    loop(NJ, lambda j: last(*piece(j)))


def reorder(up_ref, down_ref, perm_ref, out_up, out_down, perm, rows, outs, sem):
    load_perm = pltpu.make_async_copy(perm_ref, perm, sem.at[0])
    load_perm.start()
    loads, stores = [], []
    for k in range(0, D, KC):
        cols = pl.ds(k, KC)
        for stream, (src, dst) in enumerate(((up_ref, out_up), (down_ref, out_down))):
            n = len(loads)
            held = rows.at[stream, :, cols]
            loads.append(pltpu.make_async_copy(src.at[:, cols], held, sem.at[1 + n]))
            done = outs.at[stream, :, cols]
            stores.append(pltpu.make_async_copy(done, dst.at[:, cols], sem.at[1 + 2 * NK + n]))
    for load in loads:
        load.start()
    load_perm.wait()
    for n, (load, store) in enumerate(zip(loads, stores)):
        stream, cols = n % 2, pl.ds(n // 2 * KC, KC)
        load.wait()
        outs[stream, :, cols] = dot(perm[stream, :, 0:ROWS], rows[stream, :, cols]).astype(BF16)
        store.start()
    for store in stores:
        store.wait()


def local(stream_up, stream_down, norm_gain, router, w_gate, w_up, w_down, routes_up, routes_down):
    any_spec = pl.BlockSpec(memory_space=pl.ANY)
    out = jax.ShapeDtypeStruct((ROWS, D), BF16)
    rising, falling, perm = pl.pallas_call(
        kernel,
        out_shape=(out, out, jax.ShapeDtypeStruct((2, ROWS, 128), BF16)),
        in_specs=[any_spec] * 9,
        out_specs=(any_spec, any_spec, any_spec),
        scratch_shapes=[
            pltpu.VMEM((128, D), BF16),
            pltpu.VMEM((128, D), BF16),
            pltpu.VMEM((1, D), BF16),
            pltpu.VMEM((2, D), BF16),
            pltpu.VMEM((2, 1, ROWS), jnp.int32),
            pltpu.VMEM((8, ROWS, D), BF16),
            pltpu.VMEM((ROWS, D), BF16),
            pltpu.VMEM((2, D, HID), BF16),
            pltpu.VMEM((2, D, HID), BF16),
            pltpu.VMEM((4, HID, HALF), BF16),
            pltpu.VMEM((8 * ROWS, 2 * HID), BF16),
            pltpu.VMEM((8 * ROWS, 2 * HID), BF16),
            pltpu.VMEM((2 * ROWS, 4 * HID), F32),
            pltpu.VMEM((4 * ROWS, HALF), BF16),
            pltpu.VMEM((4 * ROWS, HALF), BF16),
            pltpu.VMEM((2 * ROWS, HALF), BF16),
            pltpu.VMEM((ROWS, HALF), BF16),
            pltpu.VMEM((ROWS, HALF), BF16),
            pltpu.VMEM((2 * ROWS, HALF), BF16),
            pltpu.VMEM((2, 2 * ROWS, HALF), BF16),
            pltpu.VMEM((2, ROWS, HALF), BF16),
            pltpu.VMEM((128, 128), BF16),
            pltpu.VMEM((2, ROWS, 128), BF16),
            pltpu.VMEM((128, 128), F32),
            pltpu.SemaphoreType.DMA((9,)),
            pltpu.SemaphoreType.DMA((N_SEM,)),
            pltpu.SemaphoreType.DMA((N_SEM,)),
            pltpu.SemaphoreType.REGULAR,
        ],
        compiler_params=pltpu.CompilerParams(
            collective_id=0, has_side_effects=True, vmem_limit_bytes=60 * 2**20
        ),
        name="relay",
    )(
        stream_up[0], stream_down[0], norm_gain, router[0].T, w_gate[0], w_up[0], w_down[0],
        routes_up.reshape(1, ROWS), routes_down.reshape(1, ROWS),
    )
    rising, falling = pl.pallas_call(
        reorder,
        out_shape=(out, out),
        in_specs=[any_spec] * 3,
        out_specs=(any_spec, any_spec),
        scratch_shapes=[
            pltpu.VMEM((2, ROWS, 128), BF16),
            pltpu.VMEM((2, ROWS, D), BF16),
            pltpu.VMEM((2, ROWS, D), BF16),
            pltpu.SemaphoreType.DMA((1 + 4 * NK,)),
        ],
        compiler_params=pltpu.CompilerParams(vmem_limit_bytes=60 * 2**20),
        name="reorder",
    )(rising, falling, perm)
    return rising[None], falling[None]


def solution(mesh):
    placed = (
        P("pp", "ep", None),
        P("pp", "ep", None),
        P("pp", None),
        P("pp", None, None),
        P("pp", None, "ep"),
        P("pp", None, "ep"),
        P("pp", "ep", None),
        P(None, "pp", "ep", None),
        P(None, "pp", "ep", None),
    )
    return jax.shard_map(
        local,
        mesh=mesh,
        in_specs=placed,
        out_specs=(P("pp", "ep", None), P("pp", "ep", None)),
        check_vma=False,
    )
```

```python
import jax
import jax.numpy as jnp
from jax import lax
from jax.experimental import pallas as pl
from jax.experimental.pallas import tpu as pltpu
from jax.sharding import PartitionSpec as P

MESH = pl.DeviceIdType.MESH
F32 = jnp.float32
BF16 = jnp.bfloat16
EPSILON = 1e-06
ROUTE_SCALE = 2.5

D = 7168
ROWS = 64
HID = 128
HALF = D // 2
KC = 1024
NK = D // KC
JC = 512
NJ = HALF // JC
NB = NJ - 2
NR = NB + 4
WD_FIRST = 64
KX = 3

OWN, Z_OWN, ENT, Z_ENT, X_OWN, D_OWN, X_ENT, D_ENT = range(8)

OWN_X, OWN_Z, CROSS, ENT_X, ENT_Z, FWD_OWN, FWD_ENT = range(0, 7 * NK, NK)
W_BASE = 7 * NK
WD_Z, WD_Z_MORE, WD_RELAY, WD_CORE, WG_CORE, WU_CORE = range(W_BASE, W_BASE + 6)
ACT_Z = W_BASE + 6
R_BASE = ACT_Z + 4
RET_XO, RET_XE, RET_ZO, RET_ZC, RET_C = range(R_BASE, R_BASE + 5 * NR, NR)
OUT_UP = R_BASE + 5 * NR
OUT_DN = OUT_UP + 4 * NJ
RELAY = OUT_DN + 4 * NJ
ONWARD = RELAY + 4 * NJ
PERM_UP = ONWARD + 4 * NJ
PERM_DN = PERM_UP + 1
N_SEM = PERM_DN + 1


def dot(a, b):
    return jnp.dot(a, b, preferred_element_type=F32)


def kernel(
    up_ref, down_ref, gain_ref, router_ref, wg_ref, wu_ref, wd_ref, routes_up, routes_down,
    out_up, out_dn, out_perm,
    xin, xs, gain_vm, router_vm, routes_vm, xb, fb, wg, wu, wd, actm, actz, acc, sx, rx, sz, sc, fc, fz, outb,
    via, place, perm, weight, local_sem, send_sem, recv_sem, ready,
):
    pp = lax.axis_index("pp")
    ep = lax.axis_index("ep")
    n_pp = lax.axis_size("pp")
    xi = ep // 4
    zi = (ep // 2) % 2
    ci = ep % 2

    def device(x, z, c):
        return (pp, x * 4 + z * 2 + c)

    xn = device(xi + 1 - 2 * (xi % 2), zi, ci)
    zn = device(xi, 1 - zi, ci)
    xc = device(3 - xi, zi, ci)
    xc_zn = device(3 - xi, 1 - zi, ci)
    core = device(xi, zi, 1 - ci)
    above = (lax.rem(pp + 1, n_pp), ep)
    below = (lax.rem(pp + n_pp - 1, n_pp), ep)
    expert = xi // 2

    yi = pp % 4
    falls = yi == 0

    def section(step):
        return (lax.rem(pp + n_pp + step, n_pp), ep)

    my_half = zi * HALF
    other_half = (1 - zi) * HALF

    def remote(src, dst, index, to):
        return pltpu.make_async_remote_copy(
            src_ref=src,
            dst_ref=dst,
            send_sem=send_sem.at[index],
            recv_sem=recv_sem.at[index],
            device_id=to,
            device_id_type=MESH,
        )

    def cols(k):
        return pl.ds(pl.multiple_of(k * KC, KC), KC)

    def block(slot, k):
        return xb.at[slot, :, cols(k)]

    def own_x(k):
        return remote(block(OWN, k), block(X_OWN, k), OWN_X + k, xn)

    def own_z(k):
        return remote(block(OWN, k), block(Z_OWN, k), OWN_Z + k, zn)

    def cross(k):
        return remote(fb.at[:, cols(k)], block(ENT, k), CROSS + k, xc)

    def ent_x(k):
        return remote(block(ENT, k), block(X_ENT, k), ENT_X + k, xn)

    def ent_z(k):
        return remote(block(ENT, k), block(Z_ENT, k), ENT_Z + k, zn)

    def fwd_own(k):
        return remote(block(Z_OWN, k), block(D_OWN, k), FWD_OWN + k, xn)

    def fwd_ent_x(k):
        return remote(block(Z_ENT, k), block(D_ENT, k), FWD_ENT + k, xn)

    def fwd_ent_z(k):
        return remote(block(X_ENT, k), block(D_ENT, k), FWD_ENT + k, zn)

    half_mine = pl.ds(pl.multiple_of(my_half, HALF), HALF)
    half_other = pl.ds(pl.multiple_of(other_half, HALF), HALF)
    some, more = pl.ds(0, WD_FIRST), pl.ds(WD_FIRST, HID - WD_FIRST)
    wd_z = remote(wd_ref.at[some, half_other], wd.at[2, some], WD_Z, zn)
    wd_z_more = remote(wd_ref.at[more, half_other], wd.at[2, more], WD_Z_MORE, zn)
    wd_relay = remote(wd.at[2], wd.at[3], WD_RELAY, core)
    wd_core = remote(wd_ref.at[:, half_mine], wd.at[1], WD_CORE, core)
    wg_core = remote(wg_ref, wg.at[1], WG_CORE, core)
    wu_core = remote(wu_ref, wu.at[1], WU_CORE, core)

    def act_z(pair):
        rows = pl.ds(pair * 2 * ROWS, 2 * ROWS)
        return remote(actm.at[rows], actz.at[rows], ACT_Z + pair, zn)

    def piece(j, streams=(0, 1)):
        p = j + 2 if streams == (1,) else j
        return p, j, pl.multiple_of(j * JC, JC), streams

    def span(streams, base, rows):
        return pl.ds(base + streams[0] * rows, len(streams) * rows)

    def ret_xo(p, j, at, streams):
        part = (span(streams, 0, ROWS), pl.ds(at, JC))
        return remote(sx.at[part], rx.at[part], RET_XO + p, xn)

    def ret_xe(p, j, at, streams):
        part = (span(streams, 128, ROWS), pl.ds(at, JC))
        return remote(sx.at[part], rx.at[part], RET_XE + p, xn)

    def ret_zo(p, j, at, streams):
        part = (span(streams, 0, 32), pl.ds(at, JC))
        return remote(sz.at[part], fz.at[part], RET_ZO + p, zn)

    def ret_zc(p, j, at, streams):
        part = (span(streams, ROWS, 32), pl.ds(at, JC))
        return remote(sz.at[part], fz.at[part], RET_ZC + p, xc_zn)

    def ret_c(p, j, at, streams):
        part = (span(streams, 0, 32), pl.ds(at, JC))
        return remote(sc.at[part], fc.at[part], RET_C + p, xc)

    def out_cols(at, n, half):
        start = jnp.where(half == 0, my_half, other_half) + at
        return pl.ds(pl.multiple_of(start, 128), n)

    def moved(src, dst, send, recv, to):
        return pltpu.make_async_remote_copy(
            src_ref=src,
            dst_ref=dst,
            send_sem=send_sem.at[send],
            recv_sem=recv_sem.at[recv],
            device_id=to,
            device_id_type=MESH,
        )

    def out_src(q, stream, at):
        return outb.at[q % 2, pl.ds(q // 2 * ROWS + stream * 32, 32), pl.ds(at, JC)]

    def row_at(q):
        row = q // 2 * 32
        return pl.ds(row if isinstance(q, int) else pl.multiple_of(row, 32), 32)

    def out_dst(ref, q, at):
        return ref.at[row_at(q), out_cols(at, JC, q % 2)]

    def send_up(stream, j, at, q):
        index = OUT_UP + 4 * j + q
        return moved(out_src(q, stream, at), out_dst(out_up, q, at), index, index, above)

    def send_dn(stream, j, at, q):
        index = OUT_DN + 4 * j + q
        return moved(out_src(q, stream, at), out_dst(out_dn, q, at), index, index, below)

    def turn(j, q):
        return jnp.where((j >= NB) & (q >= 2), 3, lax.rem(j + q, 4))

    def via_at(q, at):
        return via.at[q % 2, row_at(q), pl.ds(at, JC)]

    def detour(j, at, q):
        index = RELAY + 4 * j + q
        step = 3 - turn(j, q)
        to = section(jnp.where(falls, step, -step))
        return moved(out_src(q, 0, at), via_at(q, at), index, index, to)

    def arrived(j, at, q):
        index = RELAY + 4 * j + q
        return moved(via_at(q, at), via_at(q, at), index, index, above)

    def onward_up(j, at, q):
        dst = out_dst(out_up, q, at)
        index = 4 * j + q
        return moved(via_at(q, at), dst, ONWARD + index, OUT_UP + index, section(4 - yi))

    def onward_dn(j, at, q):
        dst = out_dst(out_dn, q, at)
        index = 4 * j + q
        return moved(via_at(q, at), dst, ONWARD + index, OUT_DN + index, section(-1 - yi))

    def perm_up(stream):
        return moved(perm.at[stream], out_perm.at[0], PERM_UP, PERM_UP, above)

    def perm_dn(stream):
        return moved(perm.at[stream], out_perm.at[1], PERM_DN, PERM_DN, below)

    def by_stream(act_0, act_1):
        @pl.when(falls)
        def _():
            act_0(1)
            act_1(0)

        @pl.when(~falls)
        def _():
            act_0(0)
            act_1(1)

    def loop(count, body):
        def step(k, carry):
            body(k)
            return carry

        lax.fori_loop(0, count, step, 0)

    def load_x(s, src):
        return pltpu.make_async_copy(src, xin.at[pl.ds(s * ROWS, ROWS)], local_sem.at[s])

    def load_routes(s, src):
        return pltpu.make_async_copy(src, routes_vm.at[s], local_sem.at[7 + s])

    def load_streams(first, second, routes_first, routes_second):
        load_x(0, first).start()
        load_x(1, second).start()
        load_routes(0, routes_first).start()
        load_routes(1, routes_second).start()

    @pl.when(falls)
    def _():
        load_streams(down_ref, up_ref, routes_down, routes_up)

    @pl.when(~falls)
    def _():
        load_streams(up_ref, down_ref, routes_up, routes_down)

    load_wg = pltpu.make_async_copy(wg_ref, wg.at[0], local_sem.at[2])
    load_wu = pltpu.make_async_copy(wu_ref, wu.at[0], local_sem.at[3])
    load_wd = pltpu.make_async_copy(wd_ref.at[:, half_mine], wd.at[0], local_sem.at[4])
    load_gain = pltpu.make_async_copy(gain_ref, gain_vm, local_sem.at[5])
    load_router = pltpu.make_async_copy(router_ref, router_vm, local_sem.at[6])
    load_gain.start()
    load_router.start()
    barrier = pltpu.get_barrier_semaphore()
    near = (xn, zn, xc, xc_zn, core)
    steps = (-4, -3, -2, -1, 1, 2, 3, 4)
    lower = sum((section(step)[0] < pp).astype(jnp.int32) for step in steps)
    for to in near:
        pl.semaphore_signal(barrier, inc=1, device_id=to, device_id_type=MESH)
    for step in steps:
        to = section(step)

        @pl.when(to[0] > pp)
        def _():
            pl.semaphore_signal(barrier, inc=1, device_id=to, device_id_type=MESH)


    token_r = lax.broadcasted_iota(jnp.int32, (128, 128), 0)
    token_c = lax.broadcasted_iota(jnp.int32, (128, 128), 1)
    load_routes(0, routes_up).wait()
    load_routes(1, routes_down).wait()
    chosen = jnp.concatenate([routes_vm[0], routes_vm[1]], axis=1)
    chosen = jnp.broadcast_to(chosen, (128, 128))
    mine = (chosen == expert).astype(F32)
    before = ((token_r < token_c) & (token_r // 64 == token_c // 64)).astype(F32)
    ahead = dot(mine.astype(BF16), before.astype(BF16))
    inside = (token_c % 64).astype(F32)
    stream = (token_c // 64 * 32).astype(F32)
    target = stream + jnp.where(mine > 0.5, ahead, 64.0 + inside - ahead)
    hit = (token_r.astype(F32) == target).astype(F32)
    place[...] = hit.astype(BF16)
    pl.semaphore_wait(barrier, len(near) + lower)
    for step in steps:
        to = section(step)

        @pl.when(to[0] < pp)
        def _():
            pl.semaphore_signal(ready, inc=1, device_id=to, device_id_type=MESH)

    wd_z.start()
    load_x(0, up_ref).wait()
    load_x(1, down_ref).wait()
    for copy in (wg_core, wu_core, wd_core, load_wg, load_wu, load_wd):
        copy.start()

    load_gain.wait()
    load_router.wait()

    def squares(k, total):
        part = xin[:, cols(k)].astype(F32)
        part = part * part
        for c in range(KC // 128):
            total = total + part[:, c * 128:(c + 1) * 128]
        return total

    total = lax.fori_loop(0, NK, squares, jnp.zeros((128, 128), F32))
    total = jnp.sum(total, axis=1, keepdims=True)
    inverse = lax.rsqrt(total * (1.0 / D) + EPSILON)
    weight[...] = jnp.broadcast_to(inverse, (128, 128))

    def normed(k):
        gain = gain_vm[:, cols(k)].astype(F32)
        return (xin[:, cols(k)].astype(F32) * weight[:, 0:1] * gain).astype(BF16)

    def first(k):
        moved = dot(place[...], normed(k)).astype(BF16)
        xb[OWN, :, cols(k)] = moved[:ROWS]
        fb[:, cols(k)] = moved[ROWS:]
        cross(k).start()
        own_x(k).start()
        own_z(k).start()

    loop(NK, first)

    back_to = stream * 2.0 + jnp.where(mine > 0.5, ahead, 32.0 + inside - ahead)
    back_hit = (token_r.astype(F32) == back_to).astype(F32).T.astype(BF16)
    perm[...] = jnp.zeros_like(perm)
    perm[0, :, 0:ROWS] = back_hit[:ROWS, :ROWS]
    perm[1, :, 0:ROWS] = back_hit[ROWS:, ROWS:]

    def affinity(k, carry):
        own, foreign = carry
        zero = router_vm[0:1, cols(k)].astype(F32)
        one = router_vm[1:2, cols(k)].astype(F32)
        near, far = jnp.where(expert == 0, zero, one), jnp.where(expert == 0, one, zero)
        own = own + jnp.sum(xb[OWN, :, cols(k)].astype(F32) * near, axis=1, keepdims=True)
        foreign = foreign + jnp.sum(fb[:, cols(k)].astype(F32) * far, axis=1, keepdims=True)
        xs[:, cols(k)] = dot(place[...], xin[:, cols(k)]).astype(BF16)
        return own, foreign

    empty = jnp.zeros((ROWS, 1), F32)
    own, foreign = lax.fori_loop(0, NK, affinity, (empty, empty))
    weight[0:ROWS] = jnp.broadcast_to(ROUTE_SCALE * jax.nn.sigmoid(own), (ROWS, 128))
    weight[ROWS:] = jnp.broadcast_to(ROUTE_SCALE * jax.nn.sigmoid(foreign), (ROWS, 128))

    load_wg.wait()
    load_wu.wait()
    load_wd.wait()
    wg_core.wait_recv()
    wu_core.wait_recv()

    def hidden_step(pair, k):
        rows = xb[pl.ds(2 * pair, 2), :, cols(k)].reshape(2 * ROWS, KC)
        gate = dot(rows, jnp.concatenate([wg[0, cols(k)], wg[1, cols(k)]], axis=1))
        up = dot(rows, jnp.concatenate([wu[0, cols(k)], wu[1, cols(k)]], axis=1))
        first_one = k == 0
        acc[:, 0:256] = jnp.where(first_one, 0.0, acc[:, 0:256]) + gate
        acc[:, 256:512] = jnp.where(first_one, 0.0, acc[:, 256:512]) + up

    def hidden_end(pair):
        act = jax.nn.silu(acc[:, 0:256]) * acc[:, 256:512]
        act = act.astype(BF16)
        for n, row in enumerate((0, ROWS, 32, ROWS + 32)):
            actm[pl.ds(pair * 2 * ROWS + n * 32, 32)] = act[row:row + 32]
        act_z(pair).start()

    acc[...] = jnp.zeros_like(acc)

    def second(k):
        cross(k).wait_recv()
        ent_x(k).start()
        ent_z(k).start()
        own_z(k).wait_recv()
        fwd_own(k).start()
        hidden_step(0, k)

    loop(NK, second)
    wd_z_more.start()

    @pl.when(lower < len(steps))
    def _():
        pl.semaphore_wait(ready, len(steps) - lower)

    by_stream(lambda s: perm_up(s).start(), lambda s: perm_dn(s).start())
    hidden_end(0)

    def third(k):
        ent_z(k).wait_recv()

        @pl.when(k < KX)
        def _():
            fwd_ent_x(k).start()

        hidden_step(1, k)

    loop(NK, third)
    hidden_end(1)

    def fourth(k):
        own_x(k).wait_recv()
        fwd_own(k).wait_recv()
        hidden_step(2, k)

    loop(NK, fourth)
    hidden_end(2)

    def relay(k):
        ent_x(k).wait_recv()

        @pl.when(k >= KX)
        def _():
            fwd_ent_z(k).start()

    loop(NK, relay)
    wd_z.wait_recv()
    wd_z_more.wait_recv()
    wd_relay.start()
    wd_core.wait_recv()

    def back(pair, at, streams):
        base = pair * 2 * ROWS
        far = []
        for s in streams:
            first = base + s * ROWS
            far += [actz[first + 32:first + 64], actz[first:first + 32]]
        first = base + streams[0] * ROWS
        near = actm[first:first + len(streams) * ROWS]
        left = jnp.concatenate([near, jnp.concatenate(far, axis=0)], axis=1)
        return dot(left, wd[:, :, pl.ds(at, JC)].reshape(4 * HID, JC))

    def back_o(p, j, at, streams):
        sx[span(streams, 0, ROWS), pl.ds(at, JC)] = back(2, at, streams).astype(BF16)
        ret_xo(p, j, at, streams).start()

    def back_e(p, j, at, streams):
        sx[span(streams, 128, ROWS), pl.ds(at, JC)] = back(3, at, streams).astype(BF16)
        ret_xe(p, j, at, streams).start()

    def finish(j, at, q, total, streams):
        rows = span(streams, q // 2 * ROWS, 32)
        out = xs[rows, out_cols(at, JC, q % 2)].astype(F32) + weight[rows, 0:1] * total
        outb[q % 2, rows, pl.ds(at, JC)] = out.astype(BF16)
        if 0 in streams:
            straight = (turn(j, q) == 3) | (yi == 1) | (yi == 2)

            @pl.when(straight & falls)
            def _():
                send_dn(0, j, at, q).start()

            @pl.when(straight & ~falls)
            def _():
                send_up(0, j, at, q).start()

            @pl.when(~straight)
            def _():
                detour(j, at, q).start()

        if 1 in streams:

            @pl.when(falls)
            def _():
                send_up(1, j, at, q).start()

            @pl.when(~falls)
            def _():
                send_dn(1, j, at, q).start()

    def parted(total):
        blocks = [[total[r:r + 32] for r in range(b, total.shape[0], ROWS)] for b in (0, 32)]
        return [jnp.concatenate(b, axis=0) for b in blocks]

    def sums_o(p, j, at, streams):
        total = back(0, at, streams)
        ret_xo(p, j, at, streams).wait_recv()
        total = total + rx[span(streams, 0, ROWS), pl.ds(at, JC)].astype(F32)
        mine_o, other = parted(total)
        sz[span(streams, 0, 32), pl.ds(at, JC)] = other.astype(BF16)
        ret_zo(p, j, at, streams).start()
        finish(j, at, 0, mine_o, streams)

    def sums_e(p, j, at, streams):
        total = back(1, at, streams)
        ret_xe(p, j, at, streams).wait_recv()
        total = total + rx[span(streams, 128, ROWS), pl.ds(at, JC)].astype(F32)
        mine_e, other = parted(total)
        sz[span(streams, ROWS, 32), pl.ds(at, JC)] = other.astype(BF16)
        ret_zc(p, j, at, streams).start()
        sc[span(streams, 0, 32), pl.ds(at, JC)] = mine_e.astype(BF16)
        ret_c(p, j, at, streams).start()

    def final_o(p, j, at, streams):
        ret_zo(p, j, at, streams).wait_recv()
        finish(j, at, 1, fz[span(streams, 0, 32), pl.ds(at, JC)].astype(F32), streams)

    def final_e(p, j, at, streams):
        ret_c(p, j, at, streams).wait_recv()
        finish(j, at, 2, fc[span(streams, 0, 32), pl.ds(at, JC)].astype(F32), streams)
        ret_zc(p, j, at, streams).wait_recv()
        finish(j, at, 3, fz[span(streams, ROWS, 32), pl.ds(at, JC)].astype(F32), streams)

    def relays(j):
        return lax.rem(yi + 4 * NJ - j, 4), lax.rem(3 - yi + 4 * NJ - j, 4)

    def pass_on(kind, p, j, at, streams):
        up, dn = relays(j)

        @pl.when((yi != 3) & (up // 2 == kind))
        def _():
            arrived(j, at, up).wait_recv()
            onward_up(j, at, up).start()

        @pl.when((yi != 0) & (dn // 2 == kind))
        def _():
            arrived(j, at, dn).wait_recv()
            onward_dn(j, at, dn).start()

    def fifth(k):
        fwd_ent_x(k).wait_recv()
        hidden_step(3, k)

    act_z(2).wait_recv()
    wd_relay.wait_recv()
    loop(2, lambda j: back_o(*piece(j)))
    loop(KX, fifth)
    loop(NB - 2, lambda j: back_o(*piece(j + 2)))
    act_z(0).wait_recv()
    act_z(1).wait_recv()

    def sixth(k):
        fwd_ent_z(k + KX).wait_recv()
        hidden_step(3, k + KX)

    loop(NK - KX - 1, sixth)
    sums_o(*piece(0))
    sixth(NK - KX - 1)
    hidden_end(3)
    sums_o(*piece(1))
    sums_o(*piece(2))

    def drain(k):
        own_x(k).wait_send()
        own_z(k).wait_send()
        cross(k).wait_send()
        ent_x(k).wait_send()
        ent_z(k).wait_send()
        fwd_own(k).wait_send()
        fwd_ent_x(k).wait_send()

    loop(NK, drain)
    act_z(3).wait_recv()
    first = [piece(NB, (0,)), piece(NB + 1, (0,))]
    second = [piece(NB, (1,)), piece(NB + 1, (1,))]
    loop(2, lambda j: back_e(*piece(j)))
    for part in first:
        back_o(*part)

    def step(i):
        @pl.when(i + 2 < NB)
        def _():
            back_e(*piece(i + 2))

        @pl.when(i == NB - 3)
        def _():
            for part in first:
                back_e(*part)

        @pl.when(i == NB - 2)
        def _():
            for part in second:
                back_e(*part)
            for part in second:
                back_o(*part)
            for part in first:
                sums_o(*part)

        @pl.when(i + 3 < NB)
        def _():
            sums_o(*piece(i + 3))

        final_o(*piece(i))
        sums_e(*piece(i))

        @pl.when(i >= 1)
        def _():
            final_e(*piece(i - 1))

        @pl.when(i >= 2)
        def _():
            pass_on(0, *piece(i - 2))

        @pl.when(i >= 3)
        def _():
            pass_on(1, *piece(i - 3))

    loop(NB, step)
    for part in first:
        final_o(*part)
    sums_e(*first[0])
    final_e(*piece(NB - 1))
    sums_e(*first[1])
    pass_on(0, *piece(NB - 2))
    pass_on(0, *piece(NB - 1))
    pass_on(1, *piece(NB - 3))
    pass_on(1, *piece(NB - 2))
    pass_on(0, *first[0])
    pass_on(0, *first[1])
    sums_e(*second[0])
    final_e(*first[0])
    sums_e(*second[1])
    final_e(*first[1])
    pass_on(1, *piece(NB - 1))
    sums_o(*second[0])
    sums_o(*second[1])
    final_e(*second[0])
    final_o(*second[0])
    final_e(*second[1])
    final_o(*second[1])

    for copy in (wd_z, wd_z_more, wd_relay, wd_core, wg_core, wu_core, act_z(0), act_z(1), act_z(2), act_z(3)):
        copy.wait_send()
    by_stream(lambda s: perm_up(s).wait(), lambda s: perm_dn(s).wait())

    def sent(p, j, at, streams):
        ret_xo(p, j, at, streams).wait_send()
        ret_xe(p, j, at, streams).wait_send()
        ret_zo(p, j, at, streams).wait_send()
        ret_zc(p, j, at, streams).wait_send()
        ret_c(p, j, at, streams).wait_send()

    def last(p, j, at, streams):
        up, dn = relays(j)

        @pl.when((yi != 3) & ((j < NB) | (up < 2)))
        def _():
            onward_up(j, at, up).wait_send()

        @pl.when((yi != 0) & ((j < NB) | (dn < 2)))
        def _():
            onward_dn(j, at, dn).wait_send()

        for q in range(4):
            straight = (turn(j, q) == 3) | (yi == 1) | (yi == 2)

            @pl.when(falls)
            def _():
                send_up(1, j, at, q).wait_send()

            @pl.when(~falls)
            def _():
                send_dn(1, j, at, q).wait_send()

            @pl.when(straight & falls)
            def _():
                send_dn(0, j, at, q).wait_send()

            @pl.when(straight & ~falls)
            def _():
                send_up(0, j, at, q).wait_send()

            @pl.when(~straight)
            def _():
                detour(j, at, q).wait_send()

            send_up(0, j, at, q).wait_recv()
            send_dn(0, j, at, q).wait_recv()

    loop(NB, lambda j: sent(*piece(j)))
    for part in first + second:
        sent(*part)
    loop(NJ, lambda j: last(*piece(j)))


def reorder(up_ref, down_ref, perm_ref, out_up, out_down, perm, rows, outs, sem):
    load_perm = pltpu.make_async_copy(perm_ref, perm, sem.at[0])
    load_perm.start()
    loads, stores = [], []
    for k in range(0, D, HALF):
        cols = pl.ds(k, HALF)
        for stream, (src, dst) in enumerate(((up_ref, out_up), (down_ref, out_down))):
            n = len(loads)
            held = rows.at[stream, :, cols]
            loads.append(pltpu.make_async_copy(src.at[:, cols], held, sem.at[1 + n]))
            done = outs.at[stream, :, cols]
            stores.append(pltpu.make_async_copy(done, dst.at[:, cols], sem.at[1 + 4 + n]))
    for load in loads:
        load.start()
    load_perm.wait()
    for n, (load, store) in enumerate(zip(loads, stores)):
        stream, cols = n % 2, pl.ds(n // 2 * HALF, HALF)
        load.wait()
        outs[stream, :, cols] = dot(perm[stream, :, 0:ROWS], rows[stream, :, cols]).astype(BF16)
        store.start()
    for store in stores:
        store.wait()


def local(stream_up, stream_down, norm_gain, router, w_gate, w_up, w_down, routes_up, routes_down):
    any_spec = pl.BlockSpec(memory_space=pl.ANY)
    out = jax.ShapeDtypeStruct((ROWS, D), BF16)
    rising, falling, perm = pl.pallas_call(
        kernel,
        out_shape=(out, out, jax.ShapeDtypeStruct((2, ROWS, 128), BF16)),
        in_specs=[any_spec] * 9,
        out_specs=(any_spec, any_spec, any_spec),
        scratch_shapes=[
            pltpu.VMEM((128, D), BF16),
            pltpu.VMEM((128, D), BF16),
            pltpu.VMEM((1, D), BF16),
            pltpu.VMEM((2, D), BF16),
            pltpu.VMEM((2, 1, ROWS), jnp.int32),
            pltpu.VMEM((8, ROWS, D), BF16),
            pltpu.VMEM((ROWS, D), BF16),
            pltpu.VMEM((2, D, HID), BF16),
            pltpu.VMEM((2, D, HID), BF16),
            pltpu.VMEM((4, HID, HALF), BF16),
            pltpu.VMEM((8 * ROWS, 2 * HID), BF16),
            pltpu.VMEM((8 * ROWS, 2 * HID), BF16),
            pltpu.VMEM((2 * ROWS, 4 * HID), F32),
            pltpu.VMEM((4 * ROWS, HALF), BF16),
            pltpu.VMEM((4 * ROWS, HALF), BF16),
            pltpu.VMEM((2 * ROWS, HALF), BF16),
            pltpu.VMEM((ROWS, HALF), BF16),
            pltpu.VMEM((ROWS, HALF), BF16),
            pltpu.VMEM((2 * ROWS, HALF), BF16),
            pltpu.VMEM((2, 2 * ROWS, HALF), BF16),
            pltpu.VMEM((2, ROWS, HALF), BF16),
            pltpu.VMEM((128, 128), BF16),
            pltpu.VMEM((2, ROWS, 128), BF16),
            pltpu.VMEM((128, 128), F32),
            pltpu.SemaphoreType.DMA((9,)),
            pltpu.SemaphoreType.DMA((N_SEM,)),
            pltpu.SemaphoreType.DMA((N_SEM,)),
            pltpu.SemaphoreType.REGULAR,
        ],
        compiler_params=pltpu.CompilerParams(
            collective_id=0, has_side_effects=True, vmem_limit_bytes=60 * 2**20
        ),
        name="relay",
    )(
        stream_up[0], stream_down[0], norm_gain, router[0].T, w_gate[0], w_up[0], w_down[0],
        routes_up.reshape(1, ROWS), routes_down.reshape(1, ROWS),
    )
    rising, falling = pl.pallas_call(
        reorder,
        out_shape=(out, out),
        in_specs=[any_spec] * 3,
        out_specs=(any_spec, any_spec),
        scratch_shapes=[
            pltpu.VMEM((2, ROWS, 128), BF16),
            pltpu.VMEM((2, ROWS, D), BF16),
            pltpu.VMEM((2, ROWS, D), BF16),
            pltpu.SemaphoreType.DMA((1 + 8,)),
        ],
        compiler_params=pltpu.CompilerParams(vmem_limit_bytes=60 * 2**20),
        name="reorder",
    )(rising, falling, perm)
    return rising[None], falling[None]


def solution(mesh):
    placed = (
        P("pp", "ep", None),
        P("pp", "ep", None),
        P("pp", None),
        P("pp", None, None),
        P("pp", None, "ep"),
        P("pp", None, "ep"),
        P("pp", "ep", None),
        P(None, "pp", "ep", None),
        P(None, "pp", "ep", None),
    )
    return jax.shard_map(
        local,
        mesh=mesh,
        in_specs=placed,
        out_specs=(P("pp", "ep", None), P("pp", "ep", None)),
        check_vma=False,
    )
```

```python
import jax
import jax.numpy as jnp
from jax import lax
from jax.experimental import pallas as pl
from jax.experimental.pallas import tpu as pltpu
from jax.sharding import PartitionSpec as P

MESH = pl.DeviceIdType.MESH
F32 = jnp.float32
BF16 = jnp.bfloat16
EPSILON = 1e-06
ROUTE_SCALE = 2.5

D = 7168
ROWS = 64
HID = 128
HALF = D // 2
KC = 1024
NK = D // KC
JC = 512
NJ = HALF // JC
NB = NJ - 2
NR = NB + 4
WD_FIRST = 64
KX = 3

OWN, Z_OWN, ENT, Z_ENT, X_OWN, D_OWN, X_ENT, D_ENT = range(8)

OWN_X, OWN_Z, CROSS, ENT_X, ENT_Z, FWD_OWN, FWD_ENT = range(0, 7 * NK, NK)
W_BASE = 7 * NK
WD_Z, WD_Z_MORE, WD_RELAY, WD_CORE, WG_CORE, WU_CORE = range(W_BASE, W_BASE + 6)
ACT_Z = W_BASE + 6
R_BASE = ACT_Z + 4
RET_XO, RET_XE, RET_ZO, RET_ZC, RET_C = range(R_BASE, R_BASE + 5 * NR, NR)
OUT_UP = R_BASE + 5 * NR
OUT_DN = OUT_UP + 4 * NJ
RELAY = OUT_DN + 4 * NJ
ONWARD = RELAY + 4 * NJ
PERM_UP = ONWARD + 4 * NJ
PERM_DN = PERM_UP + 1
N_SEM = PERM_DN + 1


def dot(a, b):
    return jnp.dot(a, b, preferred_element_type=F32)


def kernel(
    up_ref, down_ref, gain_ref, router_ref, wg_ref, wu_ref, wd_ref, routes_up, routes_down,
    out_up, out_dn, out_perm,
    xin, xs, gain_vm, router_vm, routes_vm, xb, fb, wg, wu, wd, actm, actz, acc, sx, rx, sz, sc, fc, fz, outb,
    via, place, perm, weight, local_sem, send_sem, recv_sem, ready,
):
    pp = lax.axis_index("pp")
    ep = lax.axis_index("ep")
    n_pp = lax.axis_size("pp")
    xi = ep // 4
    zi = (ep // 2) % 2
    ci = ep % 2

    def device(x, z, c):
        return (pp, x * 4 + z * 2 + c)

    xn = device(xi + 1 - 2 * (xi % 2), zi, ci)
    zn = device(xi, 1 - zi, ci)
    xc = device(3 - xi, zi, ci)
    xc_zn = device(3 - xi, 1 - zi, ci)
    core = device(xi, zi, 1 - ci)
    above = (lax.rem(pp + 1, n_pp), ep)
    below = (lax.rem(pp + n_pp - 1, n_pp), ep)
    expert = xi // 2

    yi = pp % 4
    falls = yi == 0

    def section(step):
        return (lax.rem(pp + n_pp + step, n_pp), ep)

    my_half = zi * HALF
    other_half = (1 - zi) * HALF

    def remote(src, dst, index, to):
        return pltpu.make_async_remote_copy(
            src_ref=src,
            dst_ref=dst,
            send_sem=send_sem.at[index],
            recv_sem=recv_sem.at[index],
            device_id=to,
            device_id_type=MESH,
        )

    def cols(k):
        return pl.ds(pl.multiple_of(k * KC, KC), KC)

    def block(slot, k):
        return xb.at[slot, :, cols(k)]

    def own_x(k):
        return remote(block(OWN, k), block(X_OWN, k), OWN_X + k, xn)

    def own_z(k):
        return remote(block(OWN, k), block(Z_OWN, k), OWN_Z + k, zn)

    def cross(k):
        return remote(fb.at[:, cols(k)], block(ENT, k), CROSS + k, xc)

    def ent_x(k):
        return remote(block(ENT, k), block(X_ENT, k), ENT_X + k, xn)

    def ent_z(k):
        return remote(block(ENT, k), block(Z_ENT, k), ENT_Z + k, zn)

    def fwd_own(k):
        return remote(block(Z_OWN, k), block(D_OWN, k), FWD_OWN + k, xn)

    def fwd_ent_x(k):
        return remote(block(Z_ENT, k), block(D_ENT, k), FWD_ENT + k, xn)

    def fwd_ent_z(k):
        return remote(block(X_ENT, k), block(D_ENT, k), FWD_ENT + k, zn)

    half_mine = pl.ds(pl.multiple_of(my_half, HALF), HALF)
    half_other = pl.ds(pl.multiple_of(other_half, HALF), HALF)
    some, more = pl.ds(0, WD_FIRST), pl.ds(WD_FIRST, HID - WD_FIRST)
    wd_z = remote(wd_ref.at[some, half_other], wd.at[2, some], WD_Z, zn)
    wd_z_more = remote(wd_ref.at[more, half_other], wd.at[2, more], WD_Z_MORE, zn)
    wd_relay = remote(wd.at[2], wd.at[3], WD_RELAY, core)
    wd_core = remote(wd_ref.at[:, half_mine], wd.at[1], WD_CORE, core)
    wg_core = remote(wg_ref, wg.at[1], WG_CORE, core)
    wu_core = remote(wu_ref, wu.at[1], WU_CORE, core)

    def act_z(pair):
        rows = pl.ds(pair * 2 * ROWS, 2 * ROWS)
        return remote(actm.at[rows], actz.at[rows], ACT_Z + pair, zn)

    def piece(j, streams=(0, 1)):
        p = j + 2 if streams == (1,) else j
        return p, j, pl.multiple_of(j * JC, JC), streams

    def span(streams, base, rows):
        return pl.ds(base + streams[0] * rows, len(streams) * rows)

    def ret_xo(p, j, at, streams):
        part = (span(streams, 0, ROWS), pl.ds(at, JC))
        return remote(sx.at[part], rx.at[part], RET_XO + p, xn)

    def ret_xe(p, j, at, streams):
        part = (span(streams, 128, ROWS), pl.ds(at, JC))
        return remote(sx.at[part], rx.at[part], RET_XE + p, xn)

    def ret_zo(p, j, at, streams):
        part = (span(streams, 0, 32), pl.ds(at, JC))
        return remote(sz.at[part], fz.at[part], RET_ZO + p, zn)

    def ret_zc(p, j, at, streams):
        part = (span(streams, ROWS, 32), pl.ds(at, JC))
        return remote(sz.at[part], fz.at[part], RET_ZC + p, xc_zn)

    def ret_c(p, j, at, streams):
        part = (span(streams, 0, 32), pl.ds(at, JC))
        return remote(sc.at[part], fc.at[part], RET_C + p, xc)

    def out_cols(at, n, half):
        start = jnp.where(half == 0, my_half, other_half) + at
        return pl.ds(pl.multiple_of(start, 128), n)

    def moved(src, dst, send, recv, to):
        return pltpu.make_async_remote_copy(
            src_ref=src,
            dst_ref=dst,
            send_sem=send_sem.at[send],
            recv_sem=recv_sem.at[recv],
            device_id=to,
            device_id_type=MESH,
        )

    def out_src(q, stream, at):
        return outb.at[q % 2, pl.ds(q // 2 * ROWS + stream * 32, 32), pl.ds(at, JC)]

    def row_at(q):
        row = q // 2 * 32
        return pl.ds(row if isinstance(q, int) else pl.multiple_of(row, 32), 32)

    def out_dst(ref, q, at):
        return ref.at[row_at(q), out_cols(at, JC, q % 2)]

    def send_up(stream, j, at, q):
        index = OUT_UP + 4 * j + q
        return moved(out_src(q, stream, at), out_dst(out_up, q, at), index, index, above)

    def send_dn(stream, j, at, q):
        index = OUT_DN + 4 * j + q
        return moved(out_src(q, stream, at), out_dst(out_dn, q, at), index, index, below)

    def turn(j, q):
        return jnp.where((j >= NB) & (q >= 2), 3, lax.rem(j + q + 3, 4))

    def via_at(q, at):
        return via.at[q % 2, row_at(q), pl.ds(at, JC)]

    def detour(j, at, q):
        index = RELAY + 4 * j + q
        step = 3 - turn(j, q)
        to = section(jnp.where(falls, step, -step))
        return moved(out_src(q, 0, at), via_at(q, at), index, index, to)

    def arrived(j, at, q):
        index = RELAY + 4 * j + q
        return moved(via_at(q, at), via_at(q, at), index, index, above)

    def onward_up(j, at, q):
        dst = out_dst(out_up, q, at)
        index = 4 * j + q
        return moved(via_at(q, at), dst, ONWARD + index, OUT_UP + index, section(4 - yi))

    def onward_dn(j, at, q):
        dst = out_dst(out_dn, q, at)
        index = 4 * j + q
        return moved(via_at(q, at), dst, ONWARD + index, OUT_DN + index, section(-1 - yi))

    def perm_up(stream):
        return moved(perm.at[stream], out_perm.at[0], PERM_UP, PERM_UP, above)

    def perm_dn(stream):
        return moved(perm.at[stream], out_perm.at[1], PERM_DN, PERM_DN, below)

    def by_stream(act_0, act_1):
        @pl.when(falls)
        def _():
            act_0(1)
            act_1(0)

        @pl.when(~falls)
        def _():
            act_0(0)
            act_1(1)

    def loop(count, body):
        def step(k, carry):
            body(k)
            return carry

        lax.fori_loop(0, count, step, 0)

    def load_x(s, src):
        return pltpu.make_async_copy(src, xin.at[pl.ds(s * ROWS, ROWS)], local_sem.at[s])

    def load_routes(s, src):
        return pltpu.make_async_copy(src, routes_vm.at[s], local_sem.at[7 + s])

    def load_streams(first, second, routes_first, routes_second):
        load_x(0, first).start()
        load_x(1, second).start()
        load_routes(0, routes_first).start()
        load_routes(1, routes_second).start()

    @pl.when(falls)
    def _():
        load_streams(down_ref, up_ref, routes_down, routes_up)

    @pl.when(~falls)
    def _():
        load_streams(up_ref, down_ref, routes_up, routes_down)

    load_wg = pltpu.make_async_copy(wg_ref, wg.at[0], local_sem.at[2])
    load_wu = pltpu.make_async_copy(wu_ref, wu.at[0], local_sem.at[3])
    load_wd = pltpu.make_async_copy(wd_ref.at[:, half_mine], wd.at[0], local_sem.at[4])
    load_gain = pltpu.make_async_copy(gain_ref, gain_vm, local_sem.at[5])
    load_router = pltpu.make_async_copy(router_ref, router_vm, local_sem.at[6])
    load_gain.start()
    load_router.start()
    barrier = pltpu.get_barrier_semaphore()
    near = (xn, zn, xc, xc_zn, core)
    steps = (-4, -3, -2, -1, 1, 2, 3, 4)
    lower = sum((section(step)[0] < pp).astype(jnp.int32) for step in steps)
    for to in near:
        pl.semaphore_signal(barrier, inc=1, device_id=to, device_id_type=MESH)
    for step in steps:
        to = section(step)

        @pl.when(to[0] > pp)
        def _():
            pl.semaphore_signal(barrier, inc=1, device_id=to, device_id_type=MESH)


    token_r = lax.broadcasted_iota(jnp.int32, (128, 128), 0)
    token_c = lax.broadcasted_iota(jnp.int32, (128, 128), 1)
    load_routes(0, routes_up).wait()
    load_routes(1, routes_down).wait()
    chosen = jnp.concatenate([routes_vm[0], routes_vm[1]], axis=1)
    chosen = jnp.broadcast_to(chosen, (128, 128))
    mine = (chosen == expert).astype(F32)
    before = ((token_r < token_c) & (token_r // 64 == token_c // 64)).astype(F32)
    ahead = dot(mine.astype(BF16), before.astype(BF16))
    inside = (token_c % 64).astype(F32)
    stream = (token_c // 64 * 32).astype(F32)
    target = stream + jnp.where(mine > 0.5, ahead, 64.0 + inside - ahead)
    hit = (token_r.astype(F32) == target).astype(F32)
    place[...] = hit.astype(BF16)
    pl.semaphore_wait(barrier, len(near) + lower)
    for step in steps:
        to = section(step)

        @pl.when(to[0] < pp)
        def _():
            pl.semaphore_signal(ready, inc=1, device_id=to, device_id_type=MESH)

    wd_z.start()
    load_x(0, up_ref).wait()
    load_x(1, down_ref).wait()
    for copy in (wg_core, wu_core, wd_core, load_wg, load_wu, load_wd):
        copy.start()

    load_gain.wait()
    load_router.wait()

    def squares(k, total):
        part = xin[:, cols(k)].astype(F32)
        part = part * part
        for c in range(KC // 128):
            total = total + part[:, c * 128:(c + 1) * 128]
        return total

    total = lax.fori_loop(0, NK, squares, jnp.zeros((128, 128), F32))
    total = jnp.sum(total, axis=1, keepdims=True)
    inverse = lax.rsqrt(total * (1.0 / D) + EPSILON)
    weight[...] = jnp.broadcast_to(inverse, (128, 128))

    def normed(k):
        gain = gain_vm[:, cols(k)].astype(F32)
        return (xin[:, cols(k)].astype(F32) * weight[:, 0:1] * gain).astype(BF16)

    def first(k):
        moved = dot(place[...], normed(k)).astype(BF16)
        xb[OWN, :, cols(k)] = moved[:ROWS]
        fb[:, cols(k)] = moved[ROWS:]
        cross(k).start()
        own_x(k).start()
        own_z(k).start()

    loop(NK, first)

    back_to = stream * 2.0 + jnp.where(mine > 0.5, ahead, 32.0 + inside - ahead)
    back_hit = (token_r.astype(F32) == back_to).astype(F32).T.astype(BF16)
    perm[...] = jnp.zeros_like(perm)
    perm[0, :, 0:ROWS] = back_hit[:ROWS, :ROWS]
    perm[1, :, 0:ROWS] = back_hit[ROWS:, ROWS:]

    def affinity(k, carry):
        own, foreign = carry
        zero = router_vm[0:1, cols(k)].astype(F32)
        one = router_vm[1:2, cols(k)].astype(F32)
        near, far = jnp.where(expert == 0, zero, one), jnp.where(expert == 0, one, zero)
        own = own + jnp.sum(xb[OWN, :, cols(k)].astype(F32) * near, axis=1, keepdims=True)
        foreign = foreign + jnp.sum(fb[:, cols(k)].astype(F32) * far, axis=1, keepdims=True)
        xs[:, cols(k)] = dot(place[...], xin[:, cols(k)]).astype(BF16)
        return own, foreign

    empty = jnp.zeros((ROWS, 1), F32)
    own, foreign = lax.fori_loop(0, NK, affinity, (empty, empty))
    weight[0:ROWS] = jnp.broadcast_to(ROUTE_SCALE * jax.nn.sigmoid(own), (ROWS, 128))
    weight[ROWS:] = jnp.broadcast_to(ROUTE_SCALE * jax.nn.sigmoid(foreign), (ROWS, 128))

    load_wg.wait()
    load_wu.wait()
    load_wd.wait()
    wg_core.wait_recv()
    wu_core.wait_recv()

    def hidden_step(pair, k):
        rows = xb[pl.ds(2 * pair, 2), :, cols(k)].reshape(2 * ROWS, KC)
        gate = dot(rows, jnp.concatenate([wg[0, cols(k)], wg[1, cols(k)]], axis=1))
        up = dot(rows, jnp.concatenate([wu[0, cols(k)], wu[1, cols(k)]], axis=1))
        first_one = k == 0
        acc[:, 0:256] = jnp.where(first_one, 0.0, acc[:, 0:256]) + gate
        acc[:, 256:512] = jnp.where(first_one, 0.0, acc[:, 256:512]) + up

    def hidden_end(pair):
        act = jax.nn.silu(acc[:, 0:256]) * acc[:, 256:512]
        act = act.astype(BF16)
        for n, row in enumerate((0, ROWS, 32, ROWS + 32)):
            actm[pl.ds(pair * 2 * ROWS + n * 32, 32)] = act[row:row + 32]
        act_z(pair).start()

    acc[...] = jnp.zeros_like(acc)

    def second(k):
        cross(k).wait_recv()
        ent_x(k).start()
        ent_z(k).start()
        own_z(k).wait_recv()
        fwd_own(k).start()
        hidden_step(0, k)

    loop(NK, second)
    wd_z_more.start()

    @pl.when(lower < len(steps))
    def _():
        pl.semaphore_wait(ready, len(steps) - lower)

    by_stream(lambda s: perm_up(s).start(), lambda s: perm_dn(s).start())
    hidden_end(0)

    def third(k):
        ent_z(k).wait_recv()

        @pl.when(k < KX)
        def _():
            fwd_ent_x(k).start()

        hidden_step(1, k)

    loop(NK, third)
    hidden_end(1)

    def fourth(k):
        own_x(k).wait_recv()
        fwd_own(k).wait_recv()
        hidden_step(2, k)

    loop(NK, fourth)
    hidden_end(2)

    def relay(k):
        ent_x(k).wait_recv()

        @pl.when(k >= KX)
        def _():
            fwd_ent_z(k).start()

    loop(NK, relay)
    wd_z.wait_recv()
    wd_z_more.wait_recv()
    wd_relay.start()
    wd_core.wait_recv()

    def back(pair, at, streams):
        base = pair * 2 * ROWS
        far = []
        for s in streams:
            first = base + s * ROWS
            far += [actz[first + 32:first + 64], actz[first:first + 32]]
        first = base + streams[0] * ROWS
        near = actm[first:first + len(streams) * ROWS]
        left = jnp.concatenate([near, jnp.concatenate(far, axis=0)], axis=1)
        return dot(left, wd[:, :, pl.ds(at, JC)].reshape(4 * HID, JC))

    def back_o(p, j, at, streams):
        sx[span(streams, 0, ROWS), pl.ds(at, JC)] = back(2, at, streams).astype(BF16)
        ret_xo(p, j, at, streams).start()

    def back_e(p, j, at, streams):
        sx[span(streams, 128, ROWS), pl.ds(at, JC)] = back(3, at, streams).astype(BF16)
        ret_xe(p, j, at, streams).start()

    def finish(j, at, q, total, streams):
        rows = span(streams, q // 2 * ROWS, 32)
        out = xs[rows, out_cols(at, JC, q % 2)].astype(F32) + weight[rows, 0:1] * total
        outb[q % 2, rows, pl.ds(at, JC)] = out.astype(BF16)
        if 0 in streams:
            straight = (turn(j, q) == 3) | (yi == 1) | (yi == 2)

            @pl.when(straight & falls)
            def _():
                send_dn(0, j, at, q).start()

            @pl.when(straight & ~falls)
            def _():
                send_up(0, j, at, q).start()

            @pl.when(~straight)
            def _():
                detour(j, at, q).start()

        if 1 in streams:

            @pl.when(falls)
            def _():
                send_up(1, j, at, q).start()

            @pl.when(~falls)
            def _():
                send_dn(1, j, at, q).start()

    def parted(total):
        blocks = [[total[r:r + 32] for r in range(b, total.shape[0], ROWS)] for b in (0, 32)]
        return [jnp.concatenate(b, axis=0) for b in blocks]

    def sums_o(p, j, at, streams):
        total = back(0, at, streams)
        ret_xo(p, j, at, streams).wait_recv()
        total = total + rx[span(streams, 0, ROWS), pl.ds(at, JC)].astype(F32)
        mine_o, other = parted(total)
        sz[span(streams, 0, 32), pl.ds(at, JC)] = other.astype(BF16)
        ret_zo(p, j, at, streams).start()
        finish(j, at, 0, mine_o, streams)

    def sums_e(p, j, at, streams):
        total = back(1, at, streams)
        ret_xe(p, j, at, streams).wait_recv()
        total = total + rx[span(streams, 128, ROWS), pl.ds(at, JC)].astype(F32)
        mine_e, other = parted(total)
        sz[span(streams, ROWS, 32), pl.ds(at, JC)] = other.astype(BF16)
        ret_zc(p, j, at, streams).start()
        sc[span(streams, 0, 32), pl.ds(at, JC)] = mine_e.astype(BF16)
        ret_c(p, j, at, streams).start()

    def final_o(p, j, at, streams):
        ret_zo(p, j, at, streams).wait_recv()
        finish(j, at, 1, fz[span(streams, 0, 32), pl.ds(at, JC)].astype(F32), streams)

    def final_e(p, j, at, streams):
        ret_c(p, j, at, streams).wait_recv()
        finish(j, at, 2, fc[span(streams, 0, 32), pl.ds(at, JC)].astype(F32), streams)
        ret_zc(p, j, at, streams).wait_recv()
        finish(j, at, 3, fz[span(streams, ROWS, 32), pl.ds(at, JC)].astype(F32), streams)

    def relays(j):
        return lax.rem(yi + 4 * NJ - j - 3, 4), lax.rem(3 - yi + 4 * NJ - j - 3, 4)

    def pass_on(kind, p, j, at, streams):
        up, dn = relays(j)

        @pl.when((yi != 3) & (up // 2 == kind))
        def _():
            arrived(j, at, up).wait_recv()
            onward_up(j, at, up).start()

        @pl.when((yi != 0) & (dn // 2 == kind))
        def _():
            arrived(j, at, dn).wait_recv()
            onward_dn(j, at, dn).start()

    def fifth(k):
        fwd_ent_x(k).wait_recv()
        hidden_step(3, k)

    act_z(2).wait_recv()
    wd_relay.wait_recv()
    loop(2, lambda j: back_o(*piece(j)))
    loop(KX, fifth)
    loop(NB - 2, lambda j: back_o(*piece(j + 2)))
    act_z(0).wait_recv()
    act_z(1).wait_recv()

    def sixth(k):
        fwd_ent_z(k + KX).wait_recv()
        hidden_step(3, k + KX)

    loop(NK - KX - 1, sixth)
    sums_o(*piece(0))
    sixth(NK - KX - 1)
    hidden_end(3)
    sums_o(*piece(1))
    sums_o(*piece(2))

    def drain(k):
        own_x(k).wait_send()
        own_z(k).wait_send()
        cross(k).wait_send()
        ent_x(k).wait_send()
        ent_z(k).wait_send()
        fwd_own(k).wait_send()
        fwd_ent_x(k).wait_send()

    loop(NK, drain)
    act_z(3).wait_recv()
    first = [piece(NB, (0,)), piece(NB + 1, (0,))]
    second = [piece(NB, (1,)), piece(NB + 1, (1,))]
    loop(2, lambda j: back_e(*piece(j)))
    for part in first:
        back_o(*part)

    def step(i):
        @pl.when(i + 2 < NB)
        def _():
            back_e(*piece(i + 2))

        @pl.when(i == NB - 3)
        def _():
            for part in first:
                back_e(*part)

        @pl.when(i == NB - 2)
        def _():
            for part in second:
                back_e(*part)
            for part in second:
                back_o(*part)
            for part in first:
                sums_o(*part)

        sums_e(*piece(i))

        @pl.when(i + 3 < NB)
        def _():
            sums_o(*piece(i + 3))

        final_o(*piece(i))

        @pl.when(i >= 1)
        def _():
            final_e(*piece(i - 1))

        @pl.when(i >= 2)
        def _():
            pass_on(0, *piece(i - 2))

        @pl.when(i >= 3)
        def _():
            pass_on(1, *piece(i - 3))

    loop(NB, step)
    for part in first:
        final_o(*part)
    sums_e(*first[0])
    final_e(*piece(NB - 1))
    sums_e(*first[1])
    pass_on(0, *piece(NB - 2))
    pass_on(0, *piece(NB - 1))
    pass_on(1, *piece(NB - 3))
    pass_on(1, *piece(NB - 2))
    pass_on(0, *first[0])
    pass_on(0, *first[1])
    sums_e(*second[0])
    final_e(*first[0])
    sums_e(*second[1])
    final_e(*first[1])
    pass_on(1, *piece(NB - 1))
    sums_o(*second[0])
    sums_o(*second[1])
    final_e(*second[0])
    final_o(*second[0])
    final_e(*second[1])
    final_o(*second[1])

    for copy in (wd_z, wd_z_more, wd_relay, wd_core, wg_core, wu_core, act_z(0), act_z(1), act_z(2), act_z(3)):
        copy.wait_send()
    by_stream(lambda s: perm_up(s).wait(), lambda s: perm_dn(s).wait())

    def sent(p, j, at, streams):
        ret_xo(p, j, at, streams).wait_send()
        ret_xe(p, j, at, streams).wait_send()
        ret_zo(p, j, at, streams).wait_send()
        ret_zc(p, j, at, streams).wait_send()
        ret_c(p, j, at, streams).wait_send()

    def last(p, j, at, streams):
        up, dn = relays(j)

        @pl.when((yi != 3) & ((j < NB) | (up < 2)))
        def _():
            onward_up(j, at, up).wait_send()

        @pl.when((yi != 0) & ((j < NB) | (dn < 2)))
        def _():
            onward_dn(j, at, dn).wait_send()

        for q in range(4):
            straight = (turn(j, q) == 3) | (yi == 1) | (yi == 2)

            @pl.when(falls)
            def _():
                send_up(1, j, at, q).wait_send()

            @pl.when(~falls)
            def _():
                send_dn(1, j, at, q).wait_send()

            @pl.when(straight & falls)
            def _():
                send_dn(0, j, at, q).wait_send()

            @pl.when(straight & ~falls)
            def _():
                send_up(0, j, at, q).wait_send()

            @pl.when(~straight)
            def _():
                detour(j, at, q).wait_send()

            send_up(0, j, at, q).wait_recv()
            send_dn(0, j, at, q).wait_recv()

    loop(NB, lambda j: sent(*piece(j)))
    for part in first + second:
        sent(*part)
    loop(NJ, lambda j: last(*piece(j)))


def reorder(up_ref, down_ref, perm_ref, out_up, out_down, perm, rows, outs, sem):
    load_perm = pltpu.make_async_copy(perm_ref, perm, sem.at[0])
    load_perm.start()
    loads, stores = [], []
    for k in range(0, D, HALF):
        cols = pl.ds(k, HALF)
        for stream, (src, dst) in enumerate(((up_ref, out_up), (down_ref, out_down))):
            n = len(loads)
            held = rows.at[stream, :, cols]
            loads.append(pltpu.make_async_copy(src.at[:, cols], held, sem.at[1 + n]))
            done = outs.at[stream, :, cols]
            stores.append(pltpu.make_async_copy(done, dst.at[:, cols], sem.at[1 + 4 + n]))
    for load in loads:
        load.start()
    load_perm.wait()
    for n, (load, store) in enumerate(zip(loads, stores)):
        stream, cols = n % 2, pl.ds(n // 2 * HALF, HALF)
        load.wait()
        outs[stream, :, cols] = dot(perm[stream, :, 0:ROWS], rows[stream, :, cols]).astype(BF16)
        store.start()
    for store in stores:
        store.wait()


def local(stream_up, stream_down, norm_gain, router, w_gate, w_up, w_down, routes_up, routes_down):
    any_spec = pl.BlockSpec(memory_space=pl.ANY)
    out = jax.ShapeDtypeStruct((ROWS, D), BF16)
    rising, falling, perm = pl.pallas_call(
        kernel,
        out_shape=(out, out, jax.ShapeDtypeStruct((2, ROWS, 128), BF16)),
        in_specs=[any_spec] * 9,
        out_specs=(any_spec, any_spec, any_spec),
        scratch_shapes=[
            pltpu.VMEM((128, D), BF16),
            pltpu.VMEM((128, D), BF16),
            pltpu.VMEM((1, D), BF16),
            pltpu.VMEM((2, D), BF16),
            pltpu.VMEM((2, 1, ROWS), jnp.int32),
            pltpu.VMEM((8, ROWS, D), BF16),
            pltpu.VMEM((ROWS, D), BF16),
            pltpu.VMEM((2, D, HID), BF16),
            pltpu.VMEM((2, D, HID), BF16),
            pltpu.VMEM((4, HID, HALF), BF16),
            pltpu.VMEM((8 * ROWS, 2 * HID), BF16),
            pltpu.VMEM((8 * ROWS, 2 * HID), BF16),
            pltpu.VMEM((2 * ROWS, 4 * HID), F32),
            pltpu.VMEM((4 * ROWS, HALF), BF16),
            pltpu.VMEM((4 * ROWS, HALF), BF16),
            pltpu.VMEM((2 * ROWS, HALF), BF16),
            pltpu.VMEM((ROWS, HALF), BF16),
            pltpu.VMEM((ROWS, HALF), BF16),
            pltpu.VMEM((2 * ROWS, HALF), BF16),
            pltpu.VMEM((2, 2 * ROWS, HALF), BF16),
            pltpu.VMEM((2, ROWS, HALF), BF16),
            pltpu.VMEM((128, 128), BF16),
            pltpu.VMEM((2, ROWS, 128), BF16),
            pltpu.VMEM((128, 128), F32),
            pltpu.SemaphoreType.DMA((9,)),
            pltpu.SemaphoreType.DMA((N_SEM,)),
            pltpu.SemaphoreType.DMA((N_SEM,)),
            pltpu.SemaphoreType.REGULAR,
        ],
        compiler_params=pltpu.CompilerParams(
            collective_id=0, has_side_effects=True, vmem_limit_bytes=60 * 2**20
        ),
        name="relay",
    )(
        stream_up[0], stream_down[0], norm_gain, router[0].T, w_gate[0], w_up[0], w_down[0],
        routes_up.reshape(1, ROWS), routes_down.reshape(1, ROWS),
    )
    rising, falling = pl.pallas_call(
        reorder,
        out_shape=(out, out),
        in_specs=[any_spec] * 3,
        out_specs=(any_spec, any_spec),
        scratch_shapes=[
            pltpu.VMEM((2, ROWS, 128), BF16),
            pltpu.VMEM((2, ROWS, D), BF16),
            pltpu.VMEM((2, ROWS, D), BF16),
            pltpu.SemaphoreType.DMA((1 + 8,)),
        ],
        compiler_params=pltpu.CompilerParams(vmem_limit_bytes=60 * 2**20),
        name="reorder",
    )(rising, falling, perm)
    return rising[None], falling[None]


def solution(mesh):
    placed = (
        P("pp", "ep", None),
        P("pp", "ep", None),
        P("pp", None),
        P("pp", None, None),
        P("pp", None, "ep"),
        P("pp", None, "ep"),
        P("pp", "ep", None),
        P(None, "pp", "ep", None),
        P(None, "pp", "ep", None),
    )
    return jax.shard_map(
        local,
        mesh=mesh,
        in_specs=placed,
        out_specs=(P("pp", "ep", None), P("pp", "ep", None)),
        check_vma=False,
    )
```
